512 devices in a mesh: ep: 128 (over x, z, core), dp: 4 (over y).
Axes of the slice: x: 4, y: 4, z: 16, core: 2. Of those that a mesh axis runs over, the one named last changes fastest.
Arguments:
- tokens: bfloat16 [2, 4096, 3584], P(None, ('dp', 'ep')), parts along dimension 1, may hold values from -6 to 6
- expert_ids: int32 [2, 4096, 2], P(None, ('dp', 'ep')), parts along dimension 1, may hold values from 0 to 15, all different within a row; in each aligned block of 8 rows (0 to 7, 8 to 15, ..., all dimensions but the last counted through in order) at most 2 rows name the same one
- gate_scores: float32 [2, 4096, 2], P(None, ('dp', 'ep')), parts along dimension 1, may hold values from 0.2 to 1
- expert_weights: bfloat16 [128, 3584, 576], P('ep')
Outputs:
- mixed: bfloat16 [2, 4096, 3584], P(None, ('dp', 'ep')), parts along dimension 1
The draws below stay inside these ranges and needn't reach their ends.
There are 4 independent parts, one for each index of `dp`. The reference program is written for one: setup_inputs(seed, part) draws one part's arguments, and reference() takes and returns one part's arrays. A program takes and returns all parts, laid end to end along the dimension named above; an argument that names none is the same for every part. Nothing has to cross between parts.
Inputs may be any that keep to these rules, and one draw needn't show every extreme that they name: `expert_ids`: each row names 2 different experts; in each micro-batch no expert is named by more than 2 of one device's 8 rows, a bound that some block reaches of them.
All inputs are finite; a program needn't handle non-finite values.
Results may differ from the reference program's by a relative error of at most 0.0057.
Values may be sent and summed in bfloat16 or wider, within the bound.
No kernel may reach another device: no remote copies, remote signals or barrier semaphores. Data moves between devices by JAX's collectives and lax.ppermute only.
A program may use at most 64 MiB of HBM per device.

```python
import math
import jax
import jax.numpy as jnp
import numpy as np
from jax import lax

D = 3584
FF = 1536
TOP = 2
MB = 2
ROWS = 8
HB = 192
EXPERTS = 16
MOST = 2
TOKENS = 1024
N_EP = 128


def draw_expert_weights(key, part):
    key = jax.random.fold_in(key, 11)
    full_shape = (N_EP, D, 3 * HB)
    column = jnp.arange(3 * HB)
    spread = jnp.where(column < 2 * HB, float(D) ** (-0.5), float(FF) ** (-0.5)).astype(jnp.float32)
    values = jax.random.normal(key, full_shape, jnp.float32)
    return (values * spread).astype(jnp.bfloat16)


def level_of(key, dims, cuts, smallest, high):
    factor_of = 1.0
    for axis_at, blocks in cuts:
        steps = jax.random.uniform(jax.random.fold_in(jax.random.fold_in(key, 6), axis_at), (blocks,), jnp.float32, smallest / len(cuts), high / len(cuts))
        factor_of = factor_of * jnp.repeat(jnp.exp(steps), dims[axis_at] // blocks).reshape((-1,) + (1,) * (len(dims) - 1 - axis_at))
    return factor_of


def routed_block(own_key, own, number, rows, count, top, reach, slope):
    ranking = jax.random.permutation(own_key, count)
    packed, ordinary = portions_of(count, rows * top, reach, slope, True), portions_of(count, rows * top, reach, slope, False)
    places = jnp.arange(count)

    def named(lengths, offset_by):
        used = int((lengths > 0).sum())
        fixed = max(1, used // 4)
        shifted = fixed + (places - fixed + offset_by * (used - fixed)) % max(1, count - fixed)
        return jnp.zeros((count,), jnp.int32).at[ranking[jnp.where(places < fixed, places, shifted)]].set(jnp.asarray(lengths, jnp.int32))

    lengths = jnp.where(number % 4 == 0, named(packed, number // 4), named(ordinary, number - number // 4 - 1))
    mixed = jax.random.permutation(jax.random.fold_in(own, 3), count)
    giver, receiver = mixed[0:count // 2 * 2:2], mixed[1:count // 2 * 2:2]
    room = jnp.minimum(lengths[giver] - 1, reach - lengths[receiver]) // 2
    room = jnp.where((giver == ranking[0]) | (receiver == ranking[0]) | (lengths[receiver] == 0), 0, jnp.maximum(room, 0))
    shifted = jax.random.randint(jax.random.fold_in(own, 4), (count // 2,), 0, 1 << 20) % (room + 1)
    lengths = lengths.at[giver].add(-shifted).at[receiver].add(shifted)
    items = jnp.searchsorted(jnp.cumsum(lengths), jnp.arange(rows * top), side="right").astype(jnp.int32)
    grid = items.reshape(top, rows).T
    grid = grid[jax.random.permutation(jax.random.fold_in(own, 1), rows)]
    offset_by = jax.random.randint(jax.random.fold_in(own, 2), (rows, 1), 0, top)
    return jnp.take_along_axis(grid, (jnp.arange(top)[None, :] + offset_by) % top, axis=1)


def portions_of(count, total, most, lean, full):
    loads = [(1 << 20) // math.isqrt(rank ** lean) + 1 for rank in range(1, count + 1)]
    largest = most if full else min(most, max(-(-total // count), total * loads[0] // sum(loads)))
    least = 1 if total - largest >= count - 1 else 0
    counts, spare = [largest] + [least] * (count - 1), total - largest - least * (count - 1)
    while spare > 0:
        movable = [i for i in range(1, count) if counts[i] < largest] or [i for i in range(1, count) if counts[i] < most]
        pool, left = sum([loads[i] for i in movable]), spare
        for i in movable:
            extra = min(most - counts[i], max(1, left * loads[i] // pool), spare)
            counts[i] = counts[i] + extra
            spare = spare - extra
    return np.array(counts)


def gaussian(stream_key, shape, deviation, bound, pieces=(), kind=jnp.bfloat16):
    factor_of = level_of(stream_key, shape, pieces, -0.22, 0.18) if pieces else 1.0
    drawn = jax.random.normal(stream_key, shape, jnp.float32) * deviation * factor_of
    return jnp.minimum(jnp.maximum(drawn, -bound), bound).astype(kind)


def setup_inputs(seed: int = 0, part: int = 0) -> dict:
    arg_keys = jax.random.split(jax.random.key(seed), 5)
    part_keys = jax.random.split(jax.random.fold_in(arg_keys[4], part), 5)
    tokens = gaussian(part_keys[0], (MB, TOKENS, D), 1.0, 6.0, ((1, 128),))
    expert_ids_keys = jax.random.split(jax.random.fold_in(part_keys[1], 1), MB * TOKENS // ROWS)
    expert_ids_turns = jax.random.permutation(jax.random.fold_in(part_keys[1], 3), MB * TOKENS // ROWS)
    expert_ids = jax.vmap(lambda own, number: routed_block(jax.random.fold_in(part_keys[1], 2), own, number, ROWS, EXPERTS, TOP, MOST, 2))(expert_ids_keys, expert_ids_turns).reshape((MB, TOKENS, TOP))
    gate_scores = jnp.clip(0.2 + 0.8 * jax.random.uniform(part_keys[2], (MB, TOKENS, TOP), jnp.float32) ** level_of(part_keys[2], (MB, TOKENS, TOP), ((1, 128),), -0.2, 0.2), 0.2, 1.0)
    expert_weights = draw_expert_weights(jax.random.fold_in(arg_keys[4], 71), part)
    return dict(tokens=tokens, expert_ids=expert_ids, gate_scores=gate_scores, expert_weights=expert_weights)


def expert_block(row_block, shard_weights, unit_count):
    projected = jnp.dot(row_block, shard_weights[:, :2 * unit_count], preferred_element_type=jnp.float32)
    hidden = (jax.nn.silu(projected[:, :unit_count]) * projected[:, unit_count:]).astype(jnp.bfloat16)
    down_part = shard_weights[:, 2 * unit_count:]
    return lax.dot_general(hidden, down_part, (((1,), (1,)), ((), ())), preferred_element_type=jnp.float32).astype(jnp.bfloat16)


def reference(tokens, expert_ids, gate_scores, expert_weights):
    shards = expert_weights.shape[0]
    model_width = tokens.shape[2]
    unit_count = expert_weights.shape[2] // 3
    group_size = FF // unit_count
    experts = shards // group_size
    all_rows = tokens.reshape(-1, model_width)
    matches = (expert_ids[..., None] == jnp.arange(experts, dtype=jnp.int32)).astype(jnp.float32)
    mix_weight = jnp.sum(matches * gate_scores[..., None], axis=2).reshape(-1, experts)
    selected = jnp.sum(matches, axis=2).reshape(-1, experts)
    limit = MOST * N_EP * MB

    def accumulate(running, inputs):
        shard_weights, shard_index = inputs
        expert = shard_index // group_size
        mask_column = lax.dynamic_slice_in_dim(selected, expert, 1, 1)[:, 0]
        weight_column = lax.dynamic_slice_in_dim(mix_weight, expert, 1, 1)[:, 0]
        rank_key = jnp.where(mask_column > 0.5, 0, 1).astype(jnp.int32)
        chosen = jnp.argsort(rank_key, stable=True)[:limit].astype(jnp.int32)
        block_out = expert_block(all_rows[chosen], shard_weights, unit_count).astype(jnp.float32)
        running = running.at[chosen].add(weight_column[chosen][:, None] * block_out)
        return running, None

    start = jnp.zeros((all_rows.shape[0], model_width), jnp.float32)
    running, _ = lax.scan(accumulate, start, (expert_weights, jnp.arange(shards, dtype=jnp.int32)))
    return running.reshape(tokens.shape).astype(jnp.bfloat16)
```

```python
import jax
import jax.numpy as jnp
from jax import lax
from jax.sharding import Mesh, PartitionSpec as P

FF = 1536
BF = jnp.bfloat16
F32 = jnp.float32
ROWS_OF = ("x", "zb")


def expert_block(rows, weights):
    units = weights.shape[1] // 3
    projected = jnp.dot(rows, weights[:, : 2 * units], preferred_element_type=F32)
    hidden = (jax.nn.silu(projected[:, :units]) * projected[:, units:]).astype(BF)
    return lax.dot_general(
        hidden, weights[:, 2 * units :], (((1,), (1,)), ((), ())), preferred_element_type=F32
    )


def on_device(tokens, expert_ids, gate_scores, expert_weights):
    batches, row_count, width = tokens.shape
    experts = lax.axis_size("x") * lax.axis_size("zb")
    line = lax.axis_size("zi")
    capacity = 2
    slots = batches * capacity
    own = expert_weights[0]
    other = lax.ppermute(own, "c", [(0, 1), (1, 0)])

    matches = (expert_ids[..., None] == jnp.arange(experts, dtype=jnp.int32)).astype(jnp.int32)
    present = jnp.sum(matches, axis=2)
    before = jnp.cumsum(present, axis=1) - present
    occurrence = jnp.sum(matches * before[:, :, None, :], axis=3)
    slot = jnp.arange(capacity, dtype=jnp.int32)
    landing = (
        (expert_ids[..., None, None] == jnp.arange(experts, dtype=jnp.int32)[:, None])
        & (occurrence[..., None, None] == slot)
    ).astype(F32)
    selector = jnp.sum(landing, axis=2)
    weighting = jnp.sum(landing * gate_scores[..., None, None], axis=2)
    packed = jnp.einsum("mres,mrd->emsd", selector.astype(BF), tokens, preferred_element_type=F32)
    packed = packed.astype(BF).reshape(experts, slots, width)

    arrived = lax.all_to_all(packed, ROWS_OF, split_axis=0, concat_axis=0, tiled=True)
    half = experts // 2
    first = lax.all_gather(arrived[:half], "zi", axis=0)
    second = lax.all_gather(arrived[half:], "zi", axis=0)
    rows = jnp.concatenate([first, second], axis=1).reshape(-1, width)
    part = (expert_block(rows, own) + expert_block(rows, other)).astype(BF)
    part = part.reshape(line, experts * slots, width)
    parts = lax.all_to_all(part, "zi", split_axis=0, concat_axis=0, tiled=True)
    summed = jnp.sum(parts, axis=0, dtype=F32).astype(BF).reshape(experts, slots, width)
    returned = lax.all_to_all(summed, ROWS_OF, split_axis=0, concat_axis=0, tiled=True)
    returned = returned.reshape(experts, batches, capacity, width).astype(F32)
    mixed = jnp.einsum("mres,emsd->mrd", weighting, returned, precision=lax.Precision.HIGHEST)
    return mixed.astype(BF)


def solution(mesh):
    fine = Mesh(mesh.devices.reshape(4, 4, 4, 2, 4), ("x", "zb", "zi", "c", "dp"))
    ep = ("x", "zb", "zi", "c")
    by_row = P(None, ("dp",) + ep, None)
    return jax.shard_map(
        on_device,
        mesh=fine,
        in_specs=(by_row, by_row, by_row, P(ep, None, None)),
        out_specs=by_row,
        check_vma=False,
    )
```

```python
import jax
import jax.numpy as jnp
from jax import lax
from jax.sharding import Mesh, PartitionSpec as P

FF = 1536
BF = jnp.bfloat16
F32 = jnp.float32
ROWS_OF = ("x", "zb")


def expert_block(rows, weights):
    units = weights.shape[1] // 3
    projected = jnp.dot(rows, weights[:, : 2 * units], preferred_element_type=F32)
    hidden = (jax.nn.silu(projected[:, :units]) * projected[:, units:]).astype(BF)
    return lax.dot_general(
        hidden, weights[:, 2 * units :], (((1,), (1,)), ((), ())), preferred_element_type=F32
    )


def on_device(tokens, expert_ids, gate_scores, expert_weights):
    batches, row_count, width = tokens.shape
    experts = lax.axis_size("x") * lax.axis_size("zb")
    line = lax.axis_size("zi")
    capacity = 2
    own = expert_weights[0]
    other = lax.ppermute(own, "c", [(0, 1), (1, 0)])

    matches = (expert_ids[..., None] == jnp.arange(experts, dtype=jnp.int32)).astype(jnp.int32)
    present = jnp.sum(matches, axis=2)
    before = jnp.cumsum(present, axis=1) - present
    occurrence = jnp.sum(matches * before[:, :, None, :], axis=3)
    slot = jnp.arange(capacity, dtype=jnp.int32)
    landing = (
        (expert_ids[..., None, None] == jnp.arange(experts, dtype=jnp.int32)[:, None])
        & (occurrence[..., None, None] == slot)
    ).astype(F32)
    selector = jnp.sum(landing, axis=2)
    weighting = jnp.sum(landing * gate_scores[..., None, None], axis=2)
    selector = selector.astype(BF)

    outs = []
    for m in range(batches):
        packed = jnp.einsum("res,rd->esd", selector[m], tokens[m], preferred_element_type=F32)
        arrived = lax.all_to_all(
            packed.astype(BF), ROWS_OF, split_axis=0, concat_axis=0, tiled=True
        )
        rows = lax.all_gather(arrived, "zi", axis=0).reshape(-1, width)
        part = (expert_block(rows, own) + expert_block(rows, other)).astype(BF)
        part = part.reshape(line, experts * capacity, width)
        parts = lax.all_to_all(part, "zi", split_axis=0, concat_axis=0, tiled=True)
        summed = jnp.sum(parts, axis=0, dtype=F32).astype(BF).reshape(experts, capacity, width)
        returned = lax.all_to_all(summed, ROWS_OF, split_axis=0, concat_axis=0, tiled=True)
        mixed = jnp.einsum(
            "res,esd->rd", weighting[m], returned.astype(F32), precision=lax.Precision.HIGHEST
        )
        outs.append(mixed.astype(BF))
    return jnp.stack(outs)


def solution(mesh):
    fine = Mesh(mesh.devices.reshape(4, 4, 4, 2, 4), ("x", "zb", "zi", "c", "dp"))
    ep = ("x", "zb", "zi", "c")
    by_row = P(None, ("dp",) + ep, None)
    return jax.shard_map(
        on_device,
        mesh=fine,
        in_specs=(by_row, by_row, by_row, P(ep, None, None)),
        out_specs=by_row,
        check_vma=False,
    )
```

```python
import jax
import jax.numpy as jnp
from jax import lax
from jax.sharding import Mesh, PartitionSpec as P

FF = 1536
BF = jnp.bfloat16
F32 = jnp.float32
ROWS_OF = ("x", "zb")
HOME = ("zi", "x", "zb")
NT = (((1,), (1,)), ((), ()))


def exchange(array, step):
    size = lax.axis_size("zi")
    return lax.ppermute(array, "zi", [(i, i ^ step) for i in range(size)])


def swap(array):
    return lax.ppermute(array, "c", [(0, 1), (1, 0)])


def hidden_of(rows, weights, units):
    projected = lax.dot_general(rows, weights, NT, preferred_element_type=F32)
    return (jax.nn.silu(projected[:, :units]) * projected[:, units:]).astype(BF)


def on_device(tokens, expert_ids, gate_scores, expert_weights):
    batches, row_count, width = tokens.shape
    experts = lax.axis_size("x") * lax.axis_size("zb")
    line = lax.axis_size("zi")
    capacity = 2
    slots = batches * capacity
    columns = width // line
    turned = expert_weights[0].T
    units = turned.shape[0] // 3
    up = turned[: 2 * units]
    down = turned[2 * units :].reshape(units, line, columns)
    place = lax.axis_index("zi")

    def for_place(at):
        return lax.dynamic_index_in_dim(down, at, 1, keepdims=False)

    pieces = [for_place(place)] + [exchange(for_place(place ^ k), k) for k in range(1, line)]
    pieces = jnp.stack(pieces)
    pieces = jnp.stack(
        [lax.dynamic_index_in_dim(pieces, place ^ k, 0, keepdims=False) for k in range(line)]
    )
    other_up = swap(up)
    down_all = jnp.concatenate([pieces, swap(pieces)], axis=1)

    matches = (expert_ids[..., None] == jnp.arange(experts, dtype=jnp.int32)).astype(jnp.int32)
    present = jnp.sum(matches, axis=2)
    before = jnp.cumsum(present, axis=1) - present
    occurrence = jnp.sum(matches * before[:, :, None, :], axis=3)
    slot = jnp.arange(capacity, dtype=jnp.int32)
    landing = (
        (expert_ids[..., None, None] == jnp.arange(experts, dtype=jnp.int32)[:, None])
        & (occurrence[..., None, None] == slot)
    ).astype(F32)
    selector = jnp.sum(landing, axis=2)
    weighting = jnp.sum(landing * gate_scores[..., None, None], axis=2)
    packed = jnp.einsum("mres,mrd->emsd", selector.astype(BF), tokens, preferred_element_type=F32)
    packed = packed.astype(BF).reshape(experts, slots, width)

    arrived = lax.all_to_all(packed, ROWS_OF, split_axis=0, concat_axis=0, tiled=True)
    half = experts // 2
    first = lax.all_gather(arrived[:half], "zi", axis=0)
    second = lax.all_gather(arrived[half:], "zi", axis=0)
    rows = jnp.concatenate([first, second], axis=1).reshape(-1, width)
    hidden = jnp.concatenate(
        [hidden_of(rows, up, units), hidden_of(rows, other_up, units)], axis=1
    )
    gathered = lax.all_gather(hidden, "zi", axis=0)
    done = jnp.einsum("zrh,zhd->rd", gathered, down_all, preferred_element_type=F32).astype(BF)
    done = done.reshape(line * experts, slots, columns)
    returned = lax.all_to_all(done, HOME, split_axis=0, concat_axis=0, tiled=True)
    returned = returned.reshape(line, experts, batches, capacity, columns).astype(F32)
    mixed = jnp.einsum("mres,zemsd->mrzd", weighting, returned, precision=lax.Precision.HIGHEST)
    return mixed.astype(BF).reshape(batches, row_count, width)


def solution(mesh):
    fine = Mesh(mesh.devices.reshape(4, 4, 4, 2, 4), ("x", "zb", "zi", "c", "dp"))
    ep = ("x", "zb", "zi", "c")
    by_row = P(None, ("dp",) + ep, None)
    return jax.shard_map(
        on_device,
        mesh=fine,
        in_specs=(by_row, by_row, by_row, P(ep, None, None)),
        out_specs=by_row,
        check_vma=False,
    )
```

```python
import jax
import jax.numpy as jnp
from jax import lax
from jax.sharding import Mesh, PartitionSpec as P

FF = 1536
BF = jnp.bfloat16
F32 = jnp.float32
ROWS_OF = ("x", "zb")
HOME = ("zi", "x", "zb")
NT = (((1,), (1,)), ((), ()))


def exchange(array, step):
    size = lax.axis_size("zi")
    return lax.ppermute(array, "zi", [(i, i ^ step) for i in range(size)])


def swap(array):
    return lax.ppermute(array, "c", [(0, 1), (1, 0)])


def hidden_of(rows, weights, units):
    projected = lax.dot_general(rows, weights, NT, preferred_element_type=F32)
    return (jax.nn.silu(projected[:, :units]) * projected[:, units:]).astype(BF)


def on_device(tokens, expert_ids, gate_scores, expert_weights):
    batches, row_count, width = tokens.shape
    experts = lax.axis_size("x") * lax.axis_size("zb")
    line = lax.axis_size("zi")
    capacity = 2
    slots = batches * capacity
    columns = width // line
    turned = expert_weights[0].T
    units = turned.shape[0] // 3
    up = turned[: 2 * units]
    place = lax.axis_index("zi")
    share = units // lax.axis_size("dp")
    down = lax.dynamic_slice_in_dim(turned, 2 * units + share * lax.axis_index("dp"), share, 0)
    down = down.reshape(share, line, columns)

    def for_place(at):
        return lax.dynamic_index_in_dim(down, at, 1, keepdims=False)

    pieces = [for_place(place)] + [exchange(for_place(place ^ k), k) for k in range(1, line)]
    pieces = jnp.stack(pieces)
    pieces = jnp.stack(
        [lax.dynamic_index_in_dim(pieces, place ^ k, 0, keepdims=False) for k in range(line)]
    )
    pieces = lax.all_gather(pieces, "dp", axis=1).reshape(line, units, columns)
    other_up = swap(up)
    down_all = jnp.concatenate([pieces, swap(pieces)], axis=1)

    matches = (expert_ids[..., None] == jnp.arange(experts, dtype=jnp.int32)).astype(jnp.int32)
    present = jnp.sum(matches, axis=2)
    before = jnp.cumsum(present, axis=1) - present
    occurrence = jnp.sum(matches * before[:, :, None, :], axis=3)
    slot = jnp.arange(capacity, dtype=jnp.int32)
    landing = (
        (expert_ids[..., None, None] == jnp.arange(experts, dtype=jnp.int32)[:, None])
        & (occurrence[..., None, None] == slot)
    ).astype(F32)
    selector = jnp.sum(landing, axis=2)
    weighting = jnp.sum(landing * gate_scores[..., None, None], axis=2)
    packed = jnp.einsum("mres,mrd->emsd", selector.astype(BF), tokens, preferred_element_type=F32)
    packed = packed.astype(BF).reshape(experts, slots, width)

    arrived = lax.all_to_all(packed, ROWS_OF, split_axis=0, concat_axis=0, tiled=True)
    half = experts // 2
    first = lax.all_gather(arrived[:half], "zi", axis=0)
    second = lax.all_gather(arrived[half:], "zi", axis=0)
    rows = jnp.concatenate([first, second], axis=1).reshape(-1, width)
    hidden = jnp.concatenate(
        [hidden_of(rows, up, units), hidden_of(rows, other_up, units)], axis=1
    )
    gathered = lax.all_gather(hidden, "zi", axis=0)
    done = jnp.einsum("zrh,zhd->rd", gathered, down_all, preferred_element_type=F32).astype(BF)
    done = done.reshape(line * experts, slots, columns)
    returned = lax.all_to_all(done, HOME, split_axis=0, concat_axis=0, tiled=True)
    returned = returned.reshape(line, experts, batches, capacity, columns).astype(F32)
    mixed = jnp.einsum("mres,zemsd->mrzd", weighting, returned, precision=lax.Precision.HIGHEST)
    return mixed.astype(BF).reshape(batches, row_count, width)


def solution(mesh):
    fine = Mesh(mesh.devices.reshape(4, 4, 4, 2, 4), ("x", "zb", "zi", "c", "dp"))
    ep = ("x", "zb", "zi", "c")
    by_row = P(None, ("dp",) + ep, None)
    return jax.shard_map(
        on_device,
        mesh=fine,
        in_specs=(by_row, by_row, by_row, P(ep, None, None)),
        out_specs=by_row,
        check_vma=False,
    )
```

```python
import jax
import jax.numpy as jnp
from jax import lax
from jax.experimental import pallas as pl
from jax.experimental.pallas import tpu as pltpu
from jax.sharding import Mesh, PartitionSpec as P

FF = 1536
BF = jnp.bfloat16
F32 = jnp.float32
ROWS_OF = ("x", "zb")
HOME = ("x", "zb", "zi")
NT = (((1,), (1,)), ((), ()))


def exchange(array, axis, step):
    size = lax.axis_size(axis)
    return lax.ppermute(array, axis, [(i, i ^ step) for i in range(size)])


def swap(array):
    return lax.ppermute(array, "c", [(0, 1), (1, 0)])


def up_kernel(first_ref, second_ref, own_ref, other_ref, out_ref, gate_ref, value_ref):
    step = pl.program_id(0)
    units = own_ref.shape[0] // 2
    half = first_ref.shape[0]

    @pl.when(step == 0)
    def _():
        gate_ref[...] = jnp.zeros_like(gate_ref)
        value_ref[...] = jnp.zeros_like(value_ref)

    gates = jnp.concatenate([own_ref[:units], other_ref[:units]], axis=0)
    values = jnp.concatenate([own_ref[units:], other_ref[units:]], axis=0)
    for at, rows_ref in ((0, first_ref), (half, second_ref)):
        rows = rows_ref[...]
        here = pl.ds(at, half)
        gate_ref[here] += lax.dot_general(rows, gates, NT, preferred_element_type=F32)
        value_ref[here] += lax.dot_general(rows, values, NT, preferred_element_type=F32)

    @pl.when(step == pl.num_programs(0) - 1)
    def _():
        gate = gate_ref[...]
        out_ref[...] = (gate / (1.0 + jnp.exp(-gate)) * value_ref[...]).astype(BF)


def hidden_of(first, second, own, other):
    half, width = first.shape
    both = other.shape[0]
    chunk = 512
    rows = pl.BlockSpec((half, chunk), lambda i: (0, i))
    weights = pl.BlockSpec((both, chunk), lambda i: (0, i))
    return pl.pallas_call(
        up_kernel,
        grid=(width // chunk,),
        in_specs=[rows, rows, weights, weights],
        out_specs=pl.BlockSpec((2 * half, both), lambda i: (0, 0)),
        out_shape=jax.ShapeDtypeStruct((2 * half, both), BF),
        scratch_shapes=[pltpu.VMEM((2 * half, both), F32), pltpu.VMEM((2 * half, both), F32)],
        compiler_params=pltpu.CompilerParams(
            dimension_semantics=("arbitrary",), vmem_limit_bytes=32 << 20
        ),
    )(first, second, own, other)


def down_kernel(place_ref, hidden_ref, own_ref, other_ref, out_ref):
    shares, line = own_ref.shape[:2]
    total = jnp.zeros(out_ref.shape, F32)
    for at in range(line):
        k = place_ref[0] ^ at
        weights = [ref[place_ref[1] ^ y, k] for ref in (own_ref, other_ref) for y in range(shares)]
        weights = jnp.concatenate(weights, axis=0)
        total += jnp.dot(hidden_ref[at], weights, preferred_element_type=F32)
    out_ref[...] = total.astype(BF)


def outputs_of(place, hidden, own, other):
    vmem = pl.BlockSpec(memory_space=pltpu.VMEM)
    return pl.pallas_call(
        down_kernel,
        in_specs=[pl.BlockSpec(memory_space=pltpu.SMEM), vmem, vmem, vmem],
        out_specs=vmem,
        out_shape=jax.ShapeDtypeStruct((hidden.shape[1], own.shape[3]), BF),
        compiler_params=pltpu.CompilerParams(vmem_limit_bytes=32 << 20),
    )(place, hidden, own, other)


def on_device(tokens, expert_ids, gate_scores, expert_weights):
    batches, row_count, width = tokens.shape
    experts = lax.axis_size("x") * lax.axis_size("zb")
    line = lax.axis_size("zi")
    capacity = 2
    slots = batches * capacity
    columns = width // line
    turned = expert_weights[0].T
    units = turned.shape[0] // 3
    up = turned[: 2 * units]
    place = lax.axis_index("zi")
    share = units // lax.axis_size("dp")
    down = lax.dynamic_slice_in_dim(turned, 2 * units + share * lax.axis_index("dp"), share, 0)
    down = down.reshape(share, line, columns)

    def for_place(at):
        return lax.dynamic_index_in_dim(down, at, 1, keepdims=False)

    pieces = [for_place(place)] + [exchange(for_place(place ^ k), "zi", k) for k in range(1, line)]
    pieces = jnp.stack(pieces)
    shares = [pieces] + [exchange(pieces, "dp", k) for k in range(1, lax.axis_size("dp"))]
    shares = jnp.stack(shares)
    other_shares = swap(shares)
    other_up = swap(up)

    matches = (expert_ids[..., None] == jnp.arange(experts, dtype=jnp.int32)).astype(jnp.int32)
    present = jnp.sum(matches, axis=2)
    before = jnp.cumsum(present, axis=1) - present
    occurrence = jnp.sum(matches * before[:, :, None, :], axis=3)
    slot = jnp.arange(capacity, dtype=jnp.int32)
    landing = (
        (expert_ids[..., None, None] == jnp.arange(experts, dtype=jnp.int32)[:, None])
        & (occurrence[..., None, None] == slot)
    ).astype(F32)
    selector = jnp.sum(landing, axis=2)
    weighting = jnp.sum(landing * gate_scores[..., None, None], axis=2)
    packed = jnp.einsum("mres,mrd->emsd", selector.astype(BF), tokens, preferred_element_type=F32)
    packed = packed.astype(BF).reshape(experts, slots, width)

    arrived = lax.all_to_all(packed, ROWS_OF, split_axis=0, concat_axis=0, tiled=True)
    half = experts // 2
    first = lax.all_gather(arrived[:half], "zi", axis=0).reshape(-1, width)
    second = lax.all_gather(arrived[half:], "zi", axis=0).reshape(-1, width)
    hidden = hidden_of(first, second, turned, other_up)
    gathered = lax.all_gather(hidden, "zi", axis=0)
    done = outputs_of(
        jnp.stack([place, lax.axis_index("dp")]).astype(jnp.int32), gathered, shares, other_shares
    )
    done = done.reshape(2, line, half, slots, columns).transpose(0, 2, 1, 3, 4)
    done = done.reshape(experts * line, slots, columns)
    returned = lax.all_to_all(done, HOME, split_axis=0, concat_axis=0, tiled=True)
    returned = returned.reshape(experts, line, batches, capacity, columns).astype(F32)
    mixed = jnp.einsum("mres,ezmsd->mrzd", weighting, returned, precision=lax.Precision.HIGHEST)
    return mixed.astype(BF).reshape(batches, row_count, width)


def solution(mesh):
    fine = Mesh(mesh.devices.reshape(4, 4, 4, 2, 4), ("x", "zb", "zi", "c", "dp"))
    ep = ("x", "zb", "zi", "c")
    by_row = P(None, ("dp",) + ep, None)
    return jax.shard_map(
        on_device,
        mesh=fine,
        in_specs=(by_row, by_row, by_row, P(ep, None, None)),
        out_specs=by_row,
        check_vma=False,
    )
```

```python
import jax
import jax.numpy as jnp
from jax import lax
from jax.experimental import pallas as pl
from jax.experimental.pallas import tpu as pltpu
from jax.sharding import Mesh, PartitionSpec as P

FF = 1536
BF = jnp.bfloat16
F32 = jnp.float32
ROWS_OF = ("x", "zb")
HOME = ("x", "zb", "zi")
NT = (((1,), (1,)), ((), ()))


def exchange(array, axis, step):
    size = lax.axis_size(axis)
    return lax.ppermute(array, axis, [(i, i ^ step) for i in range(size)])


def swap(array):
    return lax.ppermute(array, "c", [(0, 1), (1, 0)])


def pack_kernel(ids_ref, tokens_ref, out_ref):
    batches, picks, rows = ids_ref.shape
    experts, slots, width = out_ref.shape
    capacity = slots // batches
    count = experts * slots
    expert = lax.broadcasted_iota(jnp.int32, (experts, rows), 0)
    row = lax.broadcasted_iota(jnp.int32, (rows, rows), 0)
    earlier = (row < lax.broadcasted_iota(jnp.int32, (rows, rows), 1)).astype(F32)
    owner = lax.broadcasted_iota(jnp.int32, (count, experts), 0) // slots
    spread = (owner == lax.broadcasted_iota(jnp.int32, (count, experts), 1)).astype(F32)
    slot = lax.broadcasted_iota(jnp.int32, (count, rows), 0) % slots
    total = jnp.zeros((count, width), F32)
    for m in range(batches):
        ids = ids_ref[m]
        named = jnp.zeros((experts, rows), jnp.bool_)
        for k in range(picks):
            named = named | (ids[k : k + 1] == expert)
        named = named.astype(F32)
        before = jnp.dot(named, earlier, preferred_element_type=F32)
        named = jnp.dot(spread, named, preferred_element_type=F32)
        before = jnp.dot(spread, before, preferred_element_type=F32)
        here = (slot // capacity == m) & (before == (slot % capacity).astype(F32))
        pick = ((named > 0.5) & here).astype(BF)
        total += jnp.dot(pick, tokens_ref[m], preferred_element_type=F32)
    out_ref[...] = total.astype(BF).reshape(out_ref.shape)


def whole(count):
    return [pl.BlockSpec(memory_space=pltpu.VMEM)] * count


def packed_of(expert_ids, tokens, experts, slots):
    return pl.pallas_call(
        pack_kernel,
        in_specs=whole(2),
        out_specs=whole(1)[0],
        out_shape=jax.ShapeDtypeStruct((experts, slots, tokens.shape[2]), BF),
        compiler_params=pltpu.CompilerParams(vmem_limit_bytes=32 << 20),
    )(expert_ids.transpose(0, 2, 1), tokens)


def up_kernel(first_ref, second_ref, own_ref, other_ref, out_ref):
    units = own_ref.shape[0] // 3
    width = own_ref.shape[1]
    rows = [ref[...].reshape(-1, width) for ref in (first_ref, second_ref)]
    rows = jnp.concatenate(rows, axis=0)
    hidden = []
    for ref in (own_ref, other_ref):
        both = lax.dot_general(ref[: 2 * units], rows, NT, preferred_element_type=F32)
        gate = both[:units]
        hidden.append(gate / (1.0 + jnp.exp(-gate)) * both[units:])
    out_ref[...] = jnp.concatenate(hidden, axis=0).T.astype(BF)


def hidden_of(first, second, own, other):
    count = 2 * first.shape[0] * first.shape[1]
    return pl.pallas_call(
        up_kernel,
        in_specs=whole(4),
        out_specs=whole(1)[0],
        out_shape=jax.ShapeDtypeStruct((count, own.shape[0] // 3 * 2), BF),
        compiler_params=pltpu.CompilerParams(vmem_limit_bytes=48 << 20),
    )(first, second, own, other)


def down_kernel(place_ref, hidden_ref, own_ref, other_ref, out_ref):
    shares, line = own_ref.shape[:2]
    total = jnp.zeros((hidden_ref.shape[1], out_ref.shape[3]), F32)
    for at in range(line):
        k = place_ref[0] ^ at
        weights = [ref[place_ref[1] ^ y, k] for ref in (own_ref, other_ref) for y in range(shares)]
        weights = jnp.concatenate(weights, axis=0)
        total += jnp.dot(hidden_ref[at], weights, preferred_element_type=F32)
    half, slots, columns = out_ref.shape[0] // 2, out_ref.shape[2], out_ref.shape[3]
    total = total.astype(BF).reshape(2, line, half, slots, columns)
    for part in range(2):
        for at in range(line):
            out_ref[part * half : (part + 1) * half, at] = total[part, at]


def outputs_of(place, hidden, own, other, experts, slots):
    return pl.pallas_call(
        down_kernel,
        in_specs=[pl.BlockSpec(memory_space=pltpu.SMEM)] + whole(3),
        out_specs=whole(1)[0],
        out_shape=jax.ShapeDtypeStruct((experts, hidden.shape[0], slots, own.shape[3]), BF),
        compiler_params=pltpu.CompilerParams(vmem_limit_bytes=32 << 20),
    )(place, hidden, own, other)


def on_device(tokens, expert_ids, gate_scores, expert_weights):
    batches, row_count, width = tokens.shape
    experts = lax.axis_size("x") * lax.axis_size("zb")
    line = lax.axis_size("zi")
    capacity = 2
    slots = batches * capacity
    columns = width // line
    turned = expert_weights[0].T
    units = turned.shape[0] // 3
    place = lax.axis_index("zi")
    share = units // lax.axis_size("dp")
    down = lax.dynamic_slice_in_dim(turned, 2 * units + share * lax.axis_index("dp"), share, 0)
    down = down.reshape(share, line, columns)

    def for_place(at):
        return lax.dynamic_index_in_dim(down, at, 1, keepdims=False)

    pieces = [for_place(place)] + [exchange(for_place(place ^ k), "zi", k) for k in range(1, line)]
    pieces = jnp.stack(pieces)
    shares = [pieces] + [exchange(pieces, "dp", k) for k in range(1, lax.axis_size("dp"))]
    other = swap(turned)

    matches = (expert_ids[..., None] == jnp.arange(experts, dtype=jnp.int32)).astype(jnp.int32)
    present = jnp.sum(matches, axis=2)
    before = jnp.cumsum(present, axis=1) - present
    occurrence = jnp.sum(matches * before[:, :, None, :], axis=3)
    slot = jnp.arange(capacity, dtype=jnp.int32)
    landing = (
        (expert_ids[..., None, None] == jnp.arange(experts, dtype=jnp.int32)[:, None])
        & (occurrence[..., None, None] == slot)
    ).astype(F32)
    weighting = jnp.sum(landing * gate_scores[..., None, None], axis=2)
    packed = packed_of(expert_ids, tokens, experts, slots)
    arrived = lax.all_to_all(packed, ROWS_OF, split_axis=0, concat_axis=0, tiled=True)
    half = experts // 2
    first = lax.all_gather(arrived[:half], "zi", axis=0, tiled=True)
    second = lax.all_gather(arrived[half:], "zi", axis=0, tiled=True)
    mark = second[0, 0, 0]
    shares = jnp.where(mark == mark, jnp.stack(shares), jnp.zeros((), BF))
    other_shares = swap(shares)
    hidden = hidden_of(first, second, turned, other)
    gathered = lax.all_gather(hidden, "zi", axis=0)
    position = jnp.stack([place, lax.axis_index("dp")]).astype(jnp.int32)
    done = outputs_of(position, gathered, shares, other_shares, experts, slots)
    done = done.reshape(experts * line, slots, columns)
    returned = lax.all_to_all(done, HOME, split_axis=0, concat_axis=0, tiled=True)
    returned = returned.reshape(experts, line, batches, capacity, columns).astype(F32)
    mixed = jnp.einsum("mres,ezmsd->mrzd", weighting, returned, precision=lax.Precision.HIGHEST)
    return mixed.astype(BF).reshape(batches, row_count, width)


def solution(mesh):
    fine = Mesh(mesh.devices.reshape(4, 4, 4, 2, 4), ("x", "zb", "zi", "c", "dp"))
    ep = ("x", "zb", "zi", "c")
    by_row = P(None, ("dp",) + ep, None)
    return jax.shard_map(
        on_device,
        mesh=fine,
        in_specs=(by_row, by_row, by_row, P(ep, None, None)),
        out_specs=by_row,
        check_vma=False,
    )
```

```python
import jax
import jax.numpy as jnp
from jax import lax
from jax.experimental import pallas as pl
from jax.experimental.pallas import tpu as pltpu
from jax.sharding import Mesh, PartitionSpec as P

FF = 1536
BF = jnp.bfloat16
F32 = jnp.float32
ROWS_OF = ("x", "zb")
HOME = ("x", "zb", "zi")
NT = (((1,), (1,)), ((), ()))


def exchange(array, axis, step):
    size = lax.axis_size(axis)
    return lax.ppermute(array, axis, [(i, i ^ step) for i in range(size)])


def after(first, then):
    mark = first[(0,) * first.ndim]
    return jnp.where(mark == mark, then, jnp.zeros((), then.dtype))


def swap(array):
    return lax.ppermute(array, "c", [(0, 1), (1, 0)])


def pack_kernel(ids_ref, tokens_ref, out_ref):
    batches, picks, rows = ids_ref.shape
    experts, slots, width = out_ref.shape
    capacity = slots // batches
    count = experts * slots
    expert = lax.broadcasted_iota(jnp.int32, (experts, rows), 0)
    row = lax.broadcasted_iota(jnp.int32, (rows, rows), 0)
    earlier = (row < lax.broadcasted_iota(jnp.int32, (rows, rows), 1)).astype(F32)
    owner = lax.broadcasted_iota(jnp.int32, (count, experts), 0) // slots
    spread = (owner == lax.broadcasted_iota(jnp.int32, (count, experts), 1)).astype(F32)
    slot = lax.broadcasted_iota(jnp.int32, (count, rows), 0) % slots
    total = jnp.zeros((count, width), F32)
    for m in range(batches):
        ids = ids_ref[m]
        named = jnp.zeros((experts, rows), jnp.bool_)
        for k in range(picks):
            named = named | (ids[k : k + 1] == expert)
        named = named.astype(F32)
        before = jnp.dot(named, earlier, preferred_element_type=F32)
        named = jnp.dot(spread, named, preferred_element_type=F32)
        before = jnp.dot(spread, before, preferred_element_type=F32)
        here = (slot // capacity == m) & (before == (slot % capacity).astype(F32))
        pick = ((named > 0.5) & here).astype(BF)
        total += jnp.dot(pick, tokens_ref[m], preferred_element_type=F32)
    out_ref[...] = total.astype(BF).reshape(out_ref.shape)


def whole(count):
    return [pl.BlockSpec(memory_space=pltpu.VMEM)] * count


def packed_of(expert_ids, tokens, experts, slots):
    return pl.pallas_call(
        pack_kernel,
        in_specs=whole(2),
        out_specs=whole(1)[0],
        out_shape=jax.ShapeDtypeStruct((experts, slots, tokens.shape[2]), BF),
        compiler_params=pltpu.CompilerParams(vmem_limit_bytes=32 << 20),
    )(expert_ids.transpose(0, 2, 1), tokens)


def up_kernel(rows_ref, own_ref, other_ref, out_ref):
    units = own_ref.shape[0] // 2
    rows = rows_ref[...].reshape(-1, own_ref.shape[1])
    hidden = []
    for ref in (own_ref, other_ref):
        both = lax.dot_general(ref[...], rows, NT, preferred_element_type=F32)
        gate = both[:units]
        hidden.append(gate / (1.0 + jnp.exp(-gate)) * both[units:])
    out_ref[...] = jnp.concatenate(hidden, axis=0).T.astype(BF)


def hidden_of(rows, own, other):
    count = rows.shape[0] * rows.shape[1]
    return pl.pallas_call(
        up_kernel,
        in_specs=whole(3),
        out_specs=whole(1)[0],
        out_shape=jax.ShapeDtypeStruct((count, own.shape[0]), BF),
        compiler_params=pltpu.CompilerParams(vmem_limit_bytes=48 << 20),
    )(rows, own, other)


def down_kernel(place_ref, hidden_ref, own_ref, other_ref, out_ref):
    shares, line = own_ref.shape[:2]
    experts, _, slots, columns = out_ref.shape
    total = jnp.zeros((line * experts * slots, columns), F32)
    for at in range(line):
        k = place_ref[0] ^ at
        weights = [ref[place_ref[1] ^ y, k] for ref in (own_ref, other_ref) for y in range(shares)]
        weights = jnp.concatenate(weights, axis=0)
        total += jnp.dot(hidden_ref[at], weights, preferred_element_type=F32)
    total = total.astype(BF).reshape(line, experts, slots, columns)
    for p in range(line):
        out_ref[:, p] = total[p]


def outputs_of(place, hidden, own, other, experts, slots):
    return pl.pallas_call(
        down_kernel,
        in_specs=[pl.BlockSpec(memory_space=pltpu.SMEM)] + whole(3),
        out_specs=whole(1)[0],
        out_shape=jax.ShapeDtypeStruct((experts, hidden.shape[0], slots, own.shape[3]), BF),
        compiler_params=pltpu.CompilerParams(vmem_limit_bytes=32 << 20),
    )(place, hidden, own, other)


def on_device(tokens, expert_ids, gate_scores, expert_weights):
    batches, row_count, width = tokens.shape
    experts = lax.axis_size("x") * lax.axis_size("zb")
    line = lax.axis_size("zi")
    capacity = 2
    slots = batches * capacity
    columns = width // line
    turned = expert_weights[0].T
    units = turned.shape[0] // 3
    place = lax.axis_index("zi")
    share = units // lax.axis_size("dp")
    down = lax.dynamic_slice_in_dim(turned, 2 * units + share * lax.axis_index("dp"), share, 0)
    down = down.reshape(share, line, columns)

    def for_place(at):
        return lax.dynamic_index_in_dim(down, at, 1, keepdims=False)

    pieces = [for_place(place)] + [exchange(for_place(place ^ k), "zi", k) for k in range(1, line)]
    other = swap(turned)

    matches = (expert_ids[..., None] == jnp.arange(experts, dtype=jnp.int32)).astype(jnp.int32)
    present = jnp.sum(matches, axis=2)
    before = jnp.cumsum(present, axis=1) - present
    occurrence = jnp.sum(matches * before[:, :, None, :], axis=3)
    slot = jnp.arange(capacity, dtype=jnp.int32)
    landing = (
        (expert_ids[..., None, None] == jnp.arange(experts, dtype=jnp.int32)[:, None])
        & (occurrence[..., None, None] == slot)
    ).astype(F32)
    weighting = jnp.sum(landing * gate_scores[..., None, None], axis=2)
    packed = packed_of(expert_ids, tokens, experts, slots)
    arrived = lax.all_to_all(packed, ROWS_OF, split_axis=0, concat_axis=0, tiled=True)
    for piece in pieces[1:]:
        arrived = after(piece, arrived)
    pieces = jnp.stack(pieces)
    rows = jnp.broadcast_to(arrived[None], (line,) + arrived.shape)
    rows = lax.all_to_all(rows, "zi", split_axis=0, concat_axis=0, tiled=True)
    rows = rows.reshape(line * experts, slots, width)
    pieces = after(arrived, pieces)
    shares = [pieces] + [exchange(pieces, "dp", k) for k in range(1, lax.axis_size("dp"))]
    shares = jnp.stack(shares)
    other_shares = swap(shares)
    up = after(arrived, turned[: 2 * units])
    other_up = after(arrived, other[: 2 * units])
    hidden = hidden_of(rows, up, other_up)
    gathered = lax.all_gather(hidden, "zi", axis=0)
    position = jnp.stack([place, lax.axis_index("dp")]).astype(jnp.int32)
    done = outputs_of(position, gathered, shares, other_shares, experts, slots)
    done = done.reshape(experts * line, slots, columns)
    returned = lax.all_to_all(done, HOME, split_axis=0, concat_axis=0, tiled=True)
    returned = returned.reshape(experts, line, batches, capacity, columns).astype(F32)
    mixed = jnp.einsum("mres,ezmsd->mrzd", weighting, returned, precision=lax.Precision.HIGHEST)
    return mixed.astype(BF).reshape(batches, row_count, width)


def solution(mesh):
    fine = Mesh(mesh.devices.reshape(4, 4, 4, 2, 4), ("x", "zb", "zi", "c", "dp"))
    ep = ("x", "zb", "zi", "c")
    by_row = P(None, ("dp",) + ep, None)
    return jax.shard_map(
        on_device,
        mesh=fine,
        in_specs=(by_row, by_row, by_row, P(ep, None, None)),
        out_specs=by_row,
        check_vma=False,
    )
```

```python
import jax
import jax.numpy as jnp
from jax import lax
from jax.experimental import pallas as pl
from jax.experimental.pallas import tpu as pltpu
from jax.sharding import Mesh, PartitionSpec as P

FF = 1536
BF = jnp.bfloat16
F32 = jnp.float32
ROWS_OF = ("x", "zb")
HOME = ("x", "zb", "zi")
NT = (((1,), (1,)), ((), ()))


def exchange(array, axis, step):
    size = lax.axis_size(axis)
    return lax.ppermute(array, axis, [(i, i ^ step) for i in range(size)])


def swap(array):
    return lax.ppermute(array, "c", [(0, 1), (1, 0)])


def pack_kernel(ids_ref, tokens_ref, *refs):
    out_ref = refs[-1]
    batches, picks, rows = ids_ref.shape
    experts, slots, width = out_ref.shape
    capacity = slots // batches
    count = experts * slots
    expert = lax.broadcasted_iota(jnp.int32, (experts, rows), 0)
    row = lax.broadcasted_iota(jnp.int32, (rows, rows), 0)
    earlier = (row < lax.broadcasted_iota(jnp.int32, (rows, rows), 1)).astype(F32)
    owner = lax.broadcasted_iota(jnp.int32, (count, experts), 0) // slots
    spread = (owner == lax.broadcasted_iota(jnp.int32, (count, experts), 1)).astype(F32)
    slot = lax.broadcasted_iota(jnp.int32, (count, rows), 0) % slots
    total = jnp.zeros((count, width), F32)
    for m in range(batches):
        ids = ids_ref[m]
        named = jnp.zeros((experts, rows), jnp.bool_)
        for k in range(picks):
            named = named | (ids[k : k + 1] == expert)
        named = named.astype(F32)
        before = jnp.dot(named, earlier, preferred_element_type=F32)
        named = jnp.dot(spread, named, preferred_element_type=F32)
        before = jnp.dot(spread, before, preferred_element_type=F32)
        here = (slot // capacity == m) & (before == (slot % capacity).astype(F32))
        pick = ((named > 0.5) & here).astype(BF)
        total += jnp.dot(pick, tokens_ref[m], preferred_element_type=F32)
    out_ref[...] = total.astype(BF).reshape(out_ref.shape)


def whole(count):
    return [pl.BlockSpec(memory_space=pltpu.VMEM)] * count


def packed_of(expert_ids, tokens, experts, slots, earlier):
    return pl.pallas_call(
        pack_kernel,
        in_specs=whole(2) + [pl.BlockSpec(memory_space=pl.ANY)] * len(earlier),
        out_specs=whole(1)[0],
        out_shape=jax.ShapeDtypeStruct((experts, slots, tokens.shape[2]), BF),
        compiler_params=pltpu.CompilerParams(vmem_limit_bytes=32 << 20),
    )(expert_ids.transpose(0, 2, 1), tokens, *earlier)


def up_kernel(first_ref, second_ref, own_ref, other_ref, out_ref):
    units = own_ref.shape[0] // 2
    width = own_ref.shape[1]
    rows = [ref[...].reshape(-1, width) for ref in (first_ref, second_ref)]
    rows = jnp.concatenate(rows, axis=0)
    hidden = []
    for ref in (own_ref, other_ref):
        both = lax.dot_general(ref[...], rows, NT, preferred_element_type=F32)
        gate = both[:units]
        hidden.append(gate / (1.0 + jnp.exp(-gate)) * both[units:])
    out_ref[...] = jnp.concatenate(hidden, axis=0).T.astype(BF)


def hidden_of(first, second, own, other):
    count = 2 * first.shape[0] * first.shape[1]
    return pl.pallas_call(
        up_kernel,
        grid=(1,),
        in_specs=whole(3) + [pl.BlockSpec(own.shape, lambda i: (0, 0))],
        out_specs=whole(1)[0],
        out_shape=jax.ShapeDtypeStruct((count, own.shape[0]), BF),
        compiler_params=pltpu.CompilerParams(vmem_limit_bytes=48 << 20),
    )(first, second, own, other)


def down_kernel(place_ref, hidden_ref, own_ref, other_ref, out_ref):
    shares, line = own_ref.shape[:2]
    total = jnp.zeros((hidden_ref.shape[1], out_ref.shape[3]), F32)
    for at in range(line):
        k = place_ref[0] ^ at
        weights = [ref[place_ref[1] ^ y, k] for ref in (own_ref, other_ref) for y in range(shares)]
        weights = jnp.concatenate(weights, axis=0)
        total += jnp.dot(hidden_ref[at], weights, preferred_element_type=F32)
    half, slots, columns = out_ref.shape[0] // 2, out_ref.shape[2], out_ref.shape[3]
    total = total.astype(BF).reshape(2, line, half, slots, columns)
    for part in range(2):
        for at in range(line):
            out_ref[part * half : (part + 1) * half, at] = total[part, at]


def outputs_of(place, hidden, own, other, experts, slots):
    return pl.pallas_call(
        down_kernel,
        in_specs=[pl.BlockSpec(memory_space=pltpu.SMEM)] + whole(3),
        out_specs=whole(1)[0],
        out_shape=jax.ShapeDtypeStruct((experts, hidden.shape[0], slots, own.shape[3]), BF),
        compiler_params=pltpu.CompilerParams(vmem_limit_bytes=32 << 20),
    )(place, hidden, own, other)


def on_device(tokens, expert_ids, gate_scores, expert_weights):
    batches, row_count, width = tokens.shape
    experts = lax.axis_size("x") * lax.axis_size("zb")
    line = lax.axis_size("zi")
    capacity = 2
    slots = batches * capacity
    columns = width // line
    turned = expert_weights[0].T
    units = turned.shape[0] // 3
    place = lax.axis_index("zi")
    share = units // lax.axis_size("dp")
    down = lax.dynamic_slice_in_dim(turned, 2 * units + share * lax.axis_index("dp"), share, 0)
    down = down.reshape(share, line, columns)

    def for_place(at):
        return lax.dynamic_index_in_dim(down, at, 1, keepdims=False)

    pieces = [for_place(place)] + [exchange(for_place(place ^ k), "zi", k) for k in range(1, line)]
    moved = pieces[1:]
    pieces = jnp.stack(pieces)
    shares = [pieces] + [exchange(pieces, "dp", k) for k in range(1, lax.axis_size("dp"))]
    other = swap(turned)
    mark = moved[0][0, 0]
    up = jnp.where(mark == mark, turned[: 2 * units], jnp.zeros((), BF))

    matches = (expert_ids[..., None] == jnp.arange(experts, dtype=jnp.int32)).astype(jnp.int32)
    present = jnp.sum(matches, axis=2)
    before = jnp.cumsum(present, axis=1) - present
    occurrence = jnp.sum(matches * before[:, :, None, :], axis=3)
    slot = jnp.arange(capacity, dtype=jnp.int32)
    landing = (
        (expert_ids[..., None, None] == jnp.arange(experts, dtype=jnp.int32)[:, None])
        & (occurrence[..., None, None] == slot)
    ).astype(F32)
    weighting = jnp.sum(landing * gate_scores[..., None, None], axis=2)
    packed = packed_of(expert_ids, tokens, experts, slots, moved)
    arrived = lax.all_to_all(packed, ROWS_OF, split_axis=0, concat_axis=0, tiled=True)
    half = experts // 2
    first = lax.all_gather(arrived[:half], "zi", axis=0, tiled=True)
    second = lax.all_gather(arrived[half:], "zi", axis=0, tiled=True)
    shares = jnp.stack(shares)
    other_shares = swap(shares)
    hidden = hidden_of(first, second, up, other)
    gathered = lax.all_gather(hidden, "zi", axis=0)
    position = jnp.stack([place, lax.axis_index("dp")]).astype(jnp.int32)
    done = outputs_of(position, gathered, shares, other_shares, experts, slots)
    done = done.reshape(experts * line, slots, columns)
    returned = lax.all_to_all(done, HOME, split_axis=0, concat_axis=0, tiled=True)
    returned = returned.reshape(experts, line, batches, capacity, columns).astype(F32)
    mixed = jnp.einsum("mres,ezmsd->mrzd", weighting, returned, precision=lax.Precision.HIGHEST)
    return mixed.astype(BF).reshape(batches, row_count, width)


def solution(mesh):
    fine = Mesh(mesh.devices.reshape(4, 4, 4, 2, 4), ("x", "zb", "zi", "c", "dp"))
    ep = ("x", "zb", "zi", "c")
    by_row = P(None, ("dp",) + ep, None)
    return jax.shard_map(
        on_device,
        mesh=fine,
        in_specs=(by_row, by_row, by_row, P(ep, None, None)),
        out_specs=by_row,
        check_vma=False,
    )
```

```python
import jax
import jax.numpy as jnp
from jax import lax
from jax.experimental import pallas as pl
from jax.experimental.pallas import tpu as pltpu
from jax.sharding import Mesh, PartitionSpec as P

FF = 1536
BF = jnp.bfloat16
F32 = jnp.float32
ROWS_OF = ("x", "zb")
HOME = ("x", "zb", "zi")
NT = (((1,), (1,)), ((), ()))


def exchange(array, axis, step):
    size = lax.axis_size(axis)
    return lax.ppermute(array, axis, [(i, i ^ step) for i in range(size)])


def swap(array):
    return lax.ppermute(array, "c", [(0, 1), (1, 0)])


def pack_kernel(ids_ref, tokens_ref, *refs):
    out_ref = refs[-1]
    batches, picks, rows = ids_ref.shape
    experts, slots, width = out_ref.shape
    capacity = slots // batches
    count = experts * slots
    expert = lax.broadcasted_iota(jnp.int32, (experts, rows), 0)
    row = lax.broadcasted_iota(jnp.int32, (rows, rows), 0)
    earlier = (row < lax.broadcasted_iota(jnp.int32, (rows, rows), 1)).astype(F32)
    owner = lax.broadcasted_iota(jnp.int32, (count, experts), 0) // slots
    spread = (owner == lax.broadcasted_iota(jnp.int32, (count, experts), 1)).astype(F32)
    slot = lax.broadcasted_iota(jnp.int32, (count, rows), 0) % slots
    total = jnp.zeros((count, width), F32)
    for m in range(batches):
        ids = ids_ref[m]
        named = jnp.zeros((experts, rows), jnp.bool_)
        for k in range(picks):
            named = named | (ids[k : k + 1] == expert)
        named = named.astype(F32)
        before = jnp.dot(named, earlier, preferred_element_type=F32)
        named = jnp.dot(spread, named, preferred_element_type=F32)
        before = jnp.dot(spread, before, preferred_element_type=F32)
        here = (slot // capacity == m) & (before == (slot % capacity).astype(F32))
        pick = ((named > 0.5) & here).astype(BF)
        total += jnp.dot(pick, tokens_ref[m], preferred_element_type=F32)
    out_ref[...] = total.astype(BF).reshape(out_ref.shape)


def whole(count):
    return [pl.BlockSpec(memory_space=pltpu.VMEM)] * count


def packed_of(expert_ids, tokens, experts, slots, earlier):
    return pl.pallas_call(
        pack_kernel,
        in_specs=whole(2) + [pl.BlockSpec(memory_space=pl.ANY)] * len(earlier),
        out_specs=whole(1)[0],
        out_shape=jax.ShapeDtypeStruct((experts, slots, tokens.shape[2]), BF),
        compiler_params=pltpu.CompilerParams(vmem_limit_bytes=16 << 20),
    )(expert_ids.transpose(0, 2, 1), tokens, *earlier)


def up_kernel(first_ref, second_ref, own_ref, other_ref, out_ref):
    units = own_ref.shape[0] // 2
    width = own_ref.shape[1]
    rows = [ref[...].reshape(-1, width) for ref in (first_ref, second_ref)]
    rows = jnp.concatenate(rows, axis=0)
    hidden = []
    for ref in (own_ref, other_ref):
        both = lax.dot_general(ref[...], rows, NT, preferred_element_type=F32)
        gate = both[:units]
        hidden.append(gate / (1.0 + jnp.exp(-gate)) * both[units:])
    out_ref[...] = jnp.concatenate(hidden, axis=0).T.astype(BF)


def hidden_of(first, second, own, other):
    count = 2 * first.shape[0] * first.shape[1]
    return pl.pallas_call(
        up_kernel,
        grid=(1,),
        in_specs=whole(3) + [pl.BlockSpec(own.shape, lambda i: (0, 0))],
        out_specs=whole(1)[0],
        out_shape=jax.ShapeDtypeStruct((count, own.shape[0]), BF),
        compiler_params=pltpu.CompilerParams(vmem_limit_bytes=24 << 20),
    )(first, second, own, other)


def down_kernel(place_ref, hidden_ref, own_ref, other_ref, out_ref):
    shares, line = own_ref.shape[:2]
    total = jnp.zeros((hidden_ref.shape[1], out_ref.shape[3]), F32)
    for at in range(line):
        weights = [ref[place_ref[0] ^ y, at] for ref in (own_ref, other_ref) for y in range(shares)]
        weights = jnp.concatenate(weights, axis=0)
        total += jnp.dot(hidden_ref[at], weights, preferred_element_type=F32)
    half, slots, columns = out_ref.shape[0] // 2, out_ref.shape[2], out_ref.shape[3]
    total = total.astype(BF).reshape(2, line, half, slots, columns)
    for part in range(2):
        for at in range(line):
            out_ref[part * half : (part + 1) * half, at] = total[part, at]


def outputs_of(place, hidden, own, other, experts, slots):
    return pl.pallas_call(
        down_kernel,
        in_specs=[pl.BlockSpec(memory_space=pltpu.SMEM)] + whole(3),
        out_specs=whole(1)[0],
        out_shape=jax.ShapeDtypeStruct((experts, hidden.shape[0], slots, own.shape[3]), BF),
        compiler_params=pltpu.CompilerParams(vmem_limit_bytes=16 << 20),
    )(place, hidden, own, other)


def on_device(tokens, expert_ids, gate_scores, expert_weights):
    batches, row_count, width = tokens.shape
    experts = lax.axis_size("x") * lax.axis_size("zb")
    line = lax.axis_size("zi")
    capacity = 2
    slots = batches * capacity
    columns = width // line
    turned = expert_weights[0].T
    units = turned.shape[0] // 3
    share = units // lax.axis_size("dp")
    down = lax.dynamic_slice_in_dim(turned, 2 * units + share * lax.axis_index("dp"), share, 0)
    down = down.reshape(share, line, columns)

    pieces = lax.all_to_all(down.transpose(1, 0, 2), "zi", split_axis=0, concat_axis=0, tiled=True)
    shares = [pieces] + [exchange(pieces, "dp", k) for k in range(1, lax.axis_size("dp"))]
    other = swap(turned)
    mark = pieces[0, 0, 0]
    up = jnp.where(mark == mark, turned[: 2 * units], jnp.zeros((), BF))

    matches = (expert_ids[..., None] == jnp.arange(experts, dtype=jnp.int32)).astype(jnp.int32)
    present = jnp.sum(matches, axis=2)
    before = jnp.cumsum(present, axis=1) - present
    occurrence = jnp.sum(matches * before[:, :, None, :], axis=3)
    slot = jnp.arange(capacity, dtype=jnp.int32)
    landing = (
        (expert_ids[..., None, None] == jnp.arange(experts, dtype=jnp.int32)[:, None])
        & (occurrence[..., None, None] == slot)
    ).astype(F32)
    weighting = jnp.sum(landing * gate_scores[..., None, None], axis=2)
    packed = packed_of(expert_ids, tokens, experts, slots, [pieces])
    arrived = lax.all_to_all(packed, ROWS_OF, split_axis=0, concat_axis=0, tiled=True)
    half = experts // 2
    first = lax.all_gather(arrived[:half], "zi", axis=0, tiled=True)
    second = lax.all_gather(arrived[half:], "zi", axis=0, tiled=True)
    shares = jnp.stack(shares)
    other_shares = swap(shares)
    hidden = hidden_of(first, second, up, other)
    gathered = lax.all_gather(hidden, "zi", axis=0)
    position = lax.axis_index("dp").astype(jnp.int32).reshape(1)
    done = outputs_of(position, gathered, shares, other_shares, experts, slots)
    done = done.reshape(experts * line, slots, columns)
    returned = lax.all_to_all(done, HOME, split_axis=0, concat_axis=0, tiled=True)
    returned = returned.reshape(experts, line, batches, capacity, columns).astype(F32)
    mixed = jnp.einsum("mres,ezmsd->mrzd", weighting, returned, precision=lax.Precision.HIGHEST)
    return mixed.astype(BF).reshape(batches, row_count, width)


def solution(mesh):
    fine = Mesh(mesh.devices.reshape(4, 4, 4, 2, 4), ("x", "zb", "zi", "c", "dp"))
    ep = ("x", "zb", "zi", "c")
    by_row = P(None, ("dp",) + ep, None)
    return jax.shard_map(
        on_device,
        mesh=fine,
        in_specs=(by_row, by_row, by_row, P(ep, None, None)),
        out_specs=by_row,
        check_vma=False,
    )
```

```python
import jax
import jax.numpy as jnp
from jax import lax
from jax.experimental import pallas as pl
from jax.experimental.pallas import tpu as pltpu
from jax.sharding import Mesh, PartitionSpec as P

FF = 1536
BF = jnp.bfloat16
F32 = jnp.float32
ROWS_OF = ("x", "zb")
HOME = ("x", "zb", "zi")
NT = (((1,), (1,)), ((), ()))


def exchange(array, axis, step):
    size = lax.axis_size(axis)
    return lax.ppermute(array, axis, [(i, i ^ step) for i in range(size)])


def after(first, then):
    mark = first[(0,) * first.ndim]
    return jnp.where(mark == mark, then, jnp.zeros((), then.dtype))


def swap(array):
    return lax.ppermute(array, "c", [(0, 1), (1, 0)])


def pack_kernel(ids_ref, gates_ref, tokens_ref, out_ref, weights_ref):
    batches, picks, rows = ids_ref.shape
    experts, slots, width = out_ref.shape
    capacity = slots // batches
    count = experts * slots
    expert = lax.broadcasted_iota(jnp.int32, (experts, rows), 0)
    row = lax.broadcasted_iota(jnp.int32, (rows, rows), 0)
    earlier = (row < lax.broadcasted_iota(jnp.int32, (rows, rows), 1)).astype(F32)
    owner = lax.broadcasted_iota(jnp.int32, (count, experts), 0) // slots
    spread = (owner == lax.broadcasted_iota(jnp.int32, (count, experts), 1)).astype(F32)
    slot = lax.broadcasted_iota(jnp.int32, (count, rows), 0) % slots
    total = jnp.zeros((count, width), F32)
    for m in range(batches):
        ids, gates = ids_ref[m], gates_ref[m]
        named = jnp.zeros((experts, rows), jnp.bool_)
        weight = jnp.zeros((experts, rows), F32)
        for k in range(picks):
            hit = ids[k : k + 1] == expert
            named = named | hit
            weight = jnp.where(hit, gates[k : k + 1], weight)
        named = named.astype(F32)
        before = jnp.dot(named, earlier, preferred_element_type=F32)
        for s in range(capacity):
            weights_ref[m, s] = jnp.where(before == s, weight, 0.0)
        named = jnp.dot(spread, named, preferred_element_type=F32)
        before = jnp.dot(spread, before, preferred_element_type=F32)
        here = (slot // capacity == m) & (before == (slot % capacity).astype(F32))
        pick = ((named > 0.5) & here).astype(BF)
        total += jnp.dot(pick, tokens_ref[m], preferred_element_type=F32)
    out_ref[...] = total.astype(BF).reshape(out_ref.shape)


def whole(count):
    return [pl.BlockSpec(memory_space=pltpu.VMEM)] * count


def packed_of(expert_ids, gate_scores, tokens, experts, slots):
    batches, rows, width = tokens.shape
    return pl.pallas_call(
        pack_kernel,
        in_specs=whole(3),
        out_specs=whole(2),
        out_shape=[
            jax.ShapeDtypeStruct((experts, slots, width), BF),
            jax.ShapeDtypeStruct((batches, slots // batches, experts, rows), F32),
        ],
        compiler_params=pltpu.CompilerParams(vmem_limit_bytes=16 << 20),
    )(expert_ids.transpose(0, 2, 1), gate_scores.transpose(0, 2, 1), tokens)


def up_kernel(rows_ref, own_ref, other_ref, out_ref):
    units = own_ref.shape[0] // 2
    rows = rows_ref[...].reshape(-1, own_ref.shape[1])
    hidden = []
    for ref in (own_ref, other_ref):
        both = lax.dot_general(ref[...], rows, NT, preferred_element_type=F32)
        gate = both[:units]
        hidden.append(gate / (1.0 + jnp.exp(-gate)) * both[units:])
    out_ref[...] = jnp.concatenate(hidden, axis=0).T.astype(BF)


def hidden_of(rows, own, other):
    count = rows.shape[0] * rows.shape[1]
    return pl.pallas_call(
        up_kernel,
        grid=(1,),
        in_specs=whole(2) + [pl.BlockSpec(own.shape, lambda i: (0, 0))],
        out_specs=whole(1)[0],
        out_shape=jax.ShapeDtypeStruct((count, own.shape[0]), BF),
        compiler_params=pltpu.CompilerParams(vmem_limit_bytes=24 << 20),
    )(rows, own, other)


def down_kernel(place_ref, hidden_ref, own_ref, other_ref, out_ref):
    shares, line = own_ref.shape[:2]
    experts, _, slots, columns = out_ref.shape
    total = jnp.zeros((line * experts * slots, columns), F32)
    for at in range(line):
        k = place_ref[0] ^ at
        weights = [ref[place_ref[1] ^ y, k] for ref in (own_ref, other_ref) for y in range(shares)]
        weights = jnp.concatenate(weights, axis=0)
        total += jnp.dot(hidden_ref[at], weights, preferred_element_type=F32)
    total = total.astype(BF).reshape(line, experts, slots, columns)
    for p in range(line):
        out_ref[:, p] = total[p]


def outputs_of(place, hidden, own, other, experts, slots):
    return pl.pallas_call(
        down_kernel,
        in_specs=[pl.BlockSpec(memory_space=pltpu.SMEM)] + whole(3),
        out_specs=whole(1)[0],
        out_shape=jax.ShapeDtypeStruct((experts, hidden.shape[0], slots, own.shape[3]), BF),
        compiler_params=pltpu.CompilerParams(vmem_limit_bytes=16 << 20),
    )(place, hidden, own, other)


def on_device(tokens, expert_ids, gate_scores, expert_weights):
    batches, row_count, width = tokens.shape
    experts = lax.axis_size("x") * lax.axis_size("zb")
    line = lax.axis_size("zi")
    capacity = 2
    slots = batches * capacity
    columns = width // line
    turned = expert_weights[0].T
    units = turned.shape[0] // 3
    place = lax.axis_index("zi")
    share = units // lax.axis_size("dp")
    down = lax.dynamic_slice_in_dim(turned, 2 * units + share * lax.axis_index("dp"), share, 0)

    packed, weighting = packed_of(expert_ids, gate_scores, tokens, experts, slots)
    arrived = lax.all_to_all(packed, ROWS_OF, split_axis=0, concat_axis=0, tiled=True)
    rows = jnp.broadcast_to(arrived[None], (line,) + arrived.shape)
    rows = lax.all_to_all(rows, "zi", split_axis=0, concat_axis=0, tiled=True)
    rows = rows.reshape(line * experts, slots, width)

    down = after(arrived, down).reshape(share, line, columns)

    def for_place(at):
        return lax.dynamic_index_in_dim(down, at, 1, keepdims=False)

    pieces = [for_place(place)] + [exchange(for_place(place ^ k), "zi", k) for k in range(1, line)]
    pieces = jnp.stack(pieces)
    shares = [pieces] + [exchange(pieces, "dp", k) for k in range(1, lax.axis_size("dp"))]
    shares = jnp.stack(shares)
    other_shares = swap(shares)
    up = after(arrived, turned[: 2 * units])
    other = swap(turned)

    hidden = hidden_of(rows, up, other)
    gathered = lax.all_gather(hidden, "zi", axis=0)
    position = jnp.stack([place, lax.axis_index("dp")]).astype(jnp.int32)
    done = outputs_of(position, gathered, shares, other_shares, experts, slots)
    done = done.reshape(experts * line, slots, columns)
    returned = lax.all_to_all(done, HOME, split_axis=0, concat_axis=0, tiled=True)
    returned = returned.reshape(experts, line, batches, capacity, columns).astype(F32)
    mixed = jnp.einsum("mser,ezmsd->mrzd", weighting, returned, precision=lax.Precision.HIGHEST)
    return mixed.astype(BF).reshape(batches, row_count, width)


def solution(mesh):
    fine = Mesh(mesh.devices.reshape(4, 4, 4, 2, 4), ("x", "zb", "zi", "c", "dp"))
    ep = ("x", "zb", "zi", "c")
    by_row = P(None, ("dp",) + ep, None)
    return jax.shard_map(
        on_device,
        mesh=fine,
        in_specs=(by_row, by_row, by_row, P(ep, None, None)),
        out_specs=by_row,
        check_vma=False,
    )
```

```python
import jax
import jax.numpy as jnp
from jax import lax
from jax.experimental import pallas as pl
from jax.experimental.pallas import tpu as pltpu
from jax.sharding import Mesh, PartitionSpec as P

FF = 1536
BF = jnp.bfloat16
F32 = jnp.float32
HOME = ("x", "zb", "zi")
ANYWHERE = pl.BlockSpec(memory_space=pl.ANY)
NT = (((1,), (1,)), ((), ()))


def exchange(array, axis, step):
    size = lax.axis_size(axis)
    return lax.ppermute(array, axis, [(i, i ^ step) for i in range(size)])


def swap(array):
    return lax.ppermute(array, "c", [(0, 1), (1, 0)])


def pack_kernel(block_ref, _, *refs):
    rows_refs, out_ref = refs[:-1], refs[-1]
    experts, blocks, slots, width = out_ref.shape
    capacity = 2
    rows = rows_refs[0].shape[0]
    per_batch = rows * capacity // slots
    count = experts * slots
    own = block_ref[0]

    def grid(shape, axis):
        return lax.broadcasted_iota(jnp.int32, shape, axis)

    row, other = grid((rows, rows), 0), grid((rows, rows), 1)
    earlier = ((other < row) & (other // per_batch == row // per_batch)).astype(F32)
    at, slot = grid((rows, count), 0), grid((rows, count), 1)
    expert = ((slot // slots) * blocks + own).astype(F32)
    of_batch = slot % slots // capacity == at // per_batch
    nth = (slot % capacity).astype(F32)
    for k, ref in enumerate(rows_refs):
        ids = ref[:, width:].astype(F32)
        hit = ((ids[:, 0:1] == expert) | (ids[:, 1:2] == expert)).astype(F32)
        before = jnp.dot(earlier, hit, preferred_element_type=F32)
        pick = jnp.where(of_batch & (before == nth), hit, 0.0).T.astype(BF)
        packed = jnp.dot(pick, ref[:, :width], preferred_element_type=F32)
        out_ref[:, (own + blocks - k) % blocks] = packed.astype(BF).reshape(experts, slots, width)


def whole(count):
    return [pl.BlockSpec(memory_space=pltpu.VMEM)] * count


def packed_of(block, earlier, rows, experts, slots, width):
    return pl.pallas_call(
        pack_kernel,
        in_specs=[pl.BlockSpec(memory_space=pltpu.SMEM), ANYWHERE] + whole(len(rows)),
        out_specs=whole(1)[0],
        out_shape=jax.ShapeDtypeStruct((experts, len(rows), slots, width), BF),
        compiler_params=pltpu.CompilerParams(vmem_limit_bytes=16 << 20),
    )(block, earlier, *rows)


def stack_kernel(_, *refs):
    for k, ref in enumerate(refs[:-1]):
        refs[-1][k] = ref[...]


def stack_after(earlier, arrays):
    return pl.pallas_call(
        stack_kernel,
        in_specs=[ANYWHERE] + whole(len(arrays)),
        out_specs=whole(1)[0],
        out_shape=jax.ShapeDtypeStruct((len(arrays),) + arrays[0].shape, arrays[0].dtype),
        compiler_params=pltpu.CompilerParams(vmem_limit_bytes=16 << 20),
    )(earlier, *arrays)


def up_kernel(first_ref, second_ref, own_ref, other_ref, out_ref):
    units = own_ref.shape[0] // 3
    width = own_ref.shape[1]
    rows = [ref[...].reshape(-1, width) for ref in (first_ref, second_ref)]
    rows = jnp.concatenate(rows, axis=0)
    hidden = []
    for ref in (own_ref, other_ref):
        both = lax.dot_general(ref[: 2 * units], rows, NT, preferred_element_type=F32)
        gate = both[:units]
        hidden.append(gate / (1.0 + jnp.exp(-gate)) * both[units:])
    out_ref[...] = jnp.concatenate(hidden, axis=0).T.astype(BF)


def hidden_of(first, second, own, other):
    count = 2 * first.shape[0] * first.shape[1]
    both = own.shape[0] // 3 * 2
    return pl.pallas_call(
        up_kernel,
        grid=(1,),
        in_specs=whole(3) + [pl.BlockSpec((both, own.shape[1]), lambda i: (0, 0))],
        out_specs=whole(1)[0],
        out_shape=jax.ShapeDtypeStruct((count, both), BF),
        compiler_params=pltpu.CompilerParams(vmem_limit_bytes=24 << 20),
    )(first, second, own, other)


def down_kernel(place_ref, hidden_ref, own_ref, other_ref, out_ref):
    shares, line = own_ref.shape[:2]
    total = jnp.zeros((hidden_ref.shape[1], out_ref.shape[3]), F32)
    for at in range(line):
        weights = [ref[place_ref[0] ^ y, at] for ref in (own_ref, other_ref) for y in range(shares)]
        weights = jnp.concatenate(weights, axis=0)
        total += jnp.dot(hidden_ref[at], weights, preferred_element_type=F32)
    half, slots, columns = out_ref.shape[0] // 2, out_ref.shape[2], out_ref.shape[3]
    total = total.astype(BF).reshape(2, line, half, slots, columns)
    for part in range(2):
        for at in range(line):
            out_ref[part * half : (part + 1) * half, at] = total[part, at]


def outputs_of(place, hidden, own, other, experts, slots):
    return pl.pallas_call(
        down_kernel,
        in_specs=[pl.BlockSpec(memory_space=pltpu.SMEM)] + whole(3),
        out_specs=whole(1)[0],
        out_shape=jax.ShapeDtypeStruct((experts, hidden.shape[0], slots, own.shape[3]), BF),
        compiler_params=pltpu.CompilerParams(vmem_limit_bytes=16 << 20),
    )(place, hidden, own, other)


def on_device(tokens, expert_ids, gate_scores, expert_weights):
    batches, row_count, width = tokens.shape
    experts = lax.axis_size("x") * lax.axis_size("zb")
    line = lax.axis_size("zi")
    capacity = 2
    slots = batches * capacity
    columns = width // line
    turned = expert_weights[0].T
    units = turned.shape[0] // 3
    share = units // lax.axis_size("dp")
    down = lax.dynamic_slice_in_dim(turned, 2 * units + share * lax.axis_index("dp"), share, 0)
    down = down.reshape(share, line, columns)

    pieces = lax.all_to_all(down.transpose(1, 0, 2), "zi", split_axis=0, concat_axis=0, tiled=True)
    shares = [pieces] + [exchange(pieces, "dp", k) for k in range(1, lax.axis_size("dp"))]
    other = swap(turned)

    matches = (expert_ids[..., None] == jnp.arange(experts, dtype=jnp.int32)).astype(jnp.int32)
    present = jnp.sum(matches, axis=2)
    before = jnp.cumsum(present, axis=1) - present
    occurrence = jnp.sum(matches * before[:, :, None, :], axis=3)
    slot = jnp.arange(capacity, dtype=jnp.int32)
    landing = (
        (expert_ids[..., None, None] == jnp.arange(experts, dtype=jnp.int32)[:, None])
        & (occurrence[..., None, None] == slot)
    ).astype(F32)
    weighting = jnp.sum(landing * gate_scores[..., None, None], axis=2)
    blocks = lax.axis_size("zb")
    named = jnp.pad(expert_ids.reshape(-1, 2).astype(BF), ((0, 0), (0, 126)))
    sent = jnp.concatenate([tokens.reshape(-1, width), named], axis=1)
    rows = [sent] + [
        lax.ppermute(sent, "zb", [(i, (i + k) % blocks) for i in range(blocks)])
        for k in range(1, blocks)
    ]
    block = lax.axis_index("zb").astype(jnp.int32).reshape(1)
    packed = packed_of(block, pieces, rows, experts // blocks, slots, width)
    arrived = lax.all_to_all(packed, "x", split_axis=0, concat_axis=0, tiled=True)
    arrived = arrived.reshape(experts, slots, width)
    half = experts // 2
    first = lax.all_gather(arrived[:half], "zi", axis=0, tiled=True)
    second = lax.all_gather(arrived[half:], "zi", axis=0, tiled=True)
    shares = stack_after(second, shares)
    other_shares = swap(shares)
    hidden = hidden_of(first, second, turned, other)
    gathered = lax.all_gather(hidden, "zi", axis=0)
    position = lax.axis_index("dp").astype(jnp.int32).reshape(1)
    done = outputs_of(position, gathered, shares, other_shares, experts, slots)
    done = done.reshape(experts * line, slots, columns)
    returned = lax.all_to_all(done, HOME, split_axis=0, concat_axis=0, tiled=True)
    returned = returned.reshape(experts, line, batches, capacity, columns).astype(F32)
    mixed = jnp.einsum("mres,ezmsd->mrzd", weighting, returned, precision=lax.Precision.HIGHEST)
    return mixed.astype(BF).reshape(batches, row_count, width)


def solution(mesh):
    fine = Mesh(mesh.devices.reshape(4, 4, 4, 2, 4), ("x", "zb", "zi", "c", "dp"))
    ep = ("x", "zb", "zi", "c")
    by_row = P(None, ("dp",) + ep, None)
    return jax.shard_map(
        on_device,
        mesh=fine,
        in_specs=(by_row, by_row, by_row, P(ep, None, None)),
        out_specs=by_row,
        check_vma=False,
    )
```

```python
import jax
import jax.numpy as jnp
from jax import lax
from jax.experimental import pallas as pl
from jax.experimental.pallas import tpu as pltpu
from jax.sharding import Mesh, PartitionSpec as P

FF = 1536
BF = jnp.bfloat16
F32 = jnp.float32
ROWS_OF = ("x", "zb")
HOME = ("x", "zb", "zi")
ANYWHERE = pl.BlockSpec(memory_space=pl.ANY)
NT = (((1,), (1,)), ((), ()))


def exchange(array, axis, step):
    size = lax.axis_size(axis)
    return lax.ppermute(array, axis, [(i, i ^ step) for i in range(size)])


def after(first, then):
    mark = first[(0,) * first.ndim]
    return jnp.where(mark == mark, then, jnp.zeros((), then.dtype))


def swap(array):
    return lax.ppermute(array, "c", [(0, 1), (1, 0)])


def pack_kernel(ids_ref, tokens_ref, out_ref):
    batches, picks, rows = ids_ref.shape
    experts, slots, width = out_ref.shape
    capacity = slots // batches
    count = experts * slots
    expert = lax.broadcasted_iota(jnp.int32, (experts, rows), 0)
    row = lax.broadcasted_iota(jnp.int32, (rows, rows), 0)
    earlier = (row < lax.broadcasted_iota(jnp.int32, (rows, rows), 1)).astype(F32)
    owner = lax.broadcasted_iota(jnp.int32, (count, experts), 0) // slots
    spread = (owner == lax.broadcasted_iota(jnp.int32, (count, experts), 1)).astype(F32)
    slot = lax.broadcasted_iota(jnp.int32, (count, rows), 0) % slots
    total = jnp.zeros((count, width), F32)
    for m in range(batches):
        ids = ids_ref[m]
        named = jnp.zeros((experts, rows), jnp.bool_)
        for k in range(picks):
            named = named | (ids[k : k + 1] == expert)
        named = named.astype(F32)
        before = jnp.dot(named, earlier, preferred_element_type=F32)
        named = jnp.dot(spread, named, preferred_element_type=F32)
        before = jnp.dot(spread, before, preferred_element_type=F32)
        here = (slot // capacity == m) & (before == (slot % capacity).astype(F32))
        pick = ((named > 0.5) & here).astype(BF)
        total += jnp.dot(pick, tokens_ref[m], preferred_element_type=F32)
    out_ref[...] = total.astype(BF).reshape(out_ref.shape)


def whole(count):
    return [pl.BlockSpec(memory_space=pltpu.VMEM)] * count


def packed_of(expert_ids, tokens, experts, slots):
    return pl.pallas_call(
        pack_kernel,
        in_specs=whole(2),
        out_specs=whole(1)[0],
        out_shape=jax.ShapeDtypeStruct((experts, slots, tokens.shape[2]), BF),
        compiler_params=pltpu.CompilerParams(vmem_limit_bytes=16 << 20),
    )(expert_ids.transpose(0, 2, 1), tokens)


def repeat_kernel(rows_ref, *refs):
    for k in range(refs[-1].shape[0]):
        refs[-1][k] = rows_ref[...]


def repeat_after(earlier, rows, times):
    return pl.pallas_call(
        repeat_kernel,
        in_specs=whole(1) + [ANYWHERE] * len(earlier),
        out_specs=whole(1)[0],
        out_shape=jax.ShapeDtypeStruct((times,) + rows.shape, rows.dtype),
        compiler_params=pltpu.CompilerParams(vmem_limit_bytes=16 << 20),
    )(rows, *earlier)


def stack_kernel(_, *refs):
    for k, ref in enumerate(refs[:-1]):
        refs[-1][k] = ref[...]


def stack_after(earlier, arrays):
    return pl.pallas_call(
        stack_kernel,
        in_specs=[ANYWHERE] + whole(len(arrays)),
        out_specs=whole(1)[0],
        out_shape=jax.ShapeDtypeStruct((len(arrays),) + arrays[0].shape, arrays[0].dtype),
        compiler_params=pltpu.CompilerParams(vmem_limit_bytes=16 << 20),
    )(earlier, *arrays)


def up_kernel(rows_ref, own_ref, other_ref, out_ref, held_ref, arrival):
    units = own_ref.shape[0] // 2
    copy = pltpu.make_async_copy(other_ref.at[pl.ds(0, 2 * units)], held_ref, arrival)
    copy.start()
    rows = rows_ref[...].reshape(-1, own_ref.shape[1])
    hidden = []
    for ref in (own_ref, held_ref):
        if ref is held_ref:
            copy.wait()
        both = lax.dot_general(ref[...], rows, NT, preferred_element_type=F32)
        gate = both[:units]
        hidden.append(gate / (1.0 + jnp.exp(-gate)) * both[units:])
    out_ref[...] = jnp.concatenate(hidden, axis=0).T.astype(BF)


def hidden_of(rows, own, other):
    count = rows.shape[0] * rows.shape[1]
    return pl.pallas_call(
        up_kernel,
        in_specs=whole(2) + [ANYWHERE],
        out_specs=whole(1)[0],
        out_shape=jax.ShapeDtypeStruct((count, own.shape[0]), BF),
        scratch_shapes=[pltpu.VMEM(own.shape, BF), pltpu.SemaphoreType.DMA(())],
        compiler_params=pltpu.CompilerParams(vmem_limit_bytes=48 << 20),
    )(rows, own, other)


def down_kernel(place_ref, hidden_ref, own_ref, other_ref, out_ref, held_ref, arrivals):
    shares, line, share, columns = own_ref.shape
    experts, _, slots, _ = out_ref.shape
    copies = []
    for at in range(line):
        for i, ref in enumerate((own_ref, other_ref)):
            source = ref.at[:, place_ref[0] ^ at]
            copies.append(pltpu.make_async_copy(source, held_ref.at[at, i], arrivals.at[at, i]))
    for copy in copies:
        copy.start()
    total = jnp.zeros((line * experts * slots, columns), F32)
    for at in range(line):
        weights = []
        for i in range(2):
            copies[2 * at + i].wait()
            weights += [held_ref[at, i, place_ref[1] ^ y] for y in range(shares)]
        weights = jnp.concatenate(weights, axis=0)
        total += jnp.dot(hidden_ref[at], weights, preferred_element_type=F32)
    total = total.astype(BF).reshape(line, experts, slots, columns)
    for p in range(line):
        out_ref[:, p] = total[p]


def outputs_of(place, hidden, own, other, experts, slots):
    shares, line, share, columns = own.shape
    return pl.pallas_call(
        down_kernel,
        in_specs=[pl.BlockSpec(memory_space=pltpu.SMEM)] + whole(1) + [ANYWHERE] * 2,
        out_specs=whole(1)[0],
        out_shape=jax.ShapeDtypeStruct((experts, line, slots, columns), BF),
        scratch_shapes=[
            pltpu.VMEM((line, 2, shares, share, columns), BF),
            pltpu.SemaphoreType.DMA((line, 2)),
        ],
        compiler_params=pltpu.CompilerParams(vmem_limit_bytes=16 << 20),
    )(place, hidden, own, other)


def on_device(tokens, expert_ids, gate_scores, expert_weights):
    batches, row_count, width = tokens.shape
    experts = lax.axis_size("x") * lax.axis_size("zb")
    line = lax.axis_size("zi")
    capacity = 2
    slots = batches * capacity
    columns = width // line
    turned = expert_weights[0].T
    units = turned.shape[0] // 3
    place = lax.axis_index("zi")
    share = units // lax.axis_size("dp")
    down = lax.dynamic_slice_in_dim(turned, 2 * units + share * lax.axis_index("dp"), share, 0)
    down = down.reshape(share, line, columns)

    def for_place(at):
        return lax.dynamic_index_in_dim(down, at, 1, keepdims=False)

    pieces = [for_place(place)] + [exchange(for_place(place ^ k), "zi", k) for k in range(1, line)]
    other = swap(turned)

    matches = (expert_ids[..., None] == jnp.arange(experts, dtype=jnp.int32)).astype(jnp.int32)
    present = jnp.sum(matches, axis=2)
    before = jnp.cumsum(present, axis=1) - present
    occurrence = jnp.sum(matches * before[:, :, None, :], axis=3)
    slot = jnp.arange(capacity, dtype=jnp.int32)
    landing = (
        (expert_ids[..., None, None] == jnp.arange(experts, dtype=jnp.int32)[:, None])
        & (occurrence[..., None, None] == slot)
    ).astype(F32)
    weighting = jnp.sum(landing * gate_scores[..., None, None], axis=2)
    packed = packed_of(expert_ids, tokens, experts, slots)
    arrived = lax.all_to_all(packed, ROWS_OF, split_axis=0, concat_axis=0, tiled=True)
    sent = repeat_after(pieces[1:], arrived, line)
    rows = lax.all_to_all(sent, "zi", split_axis=0, concat_axis=0, tiled=True)
    rows = rows.reshape(line * experts, slots, width)
    pieces = stack_after(sent, pieces)
    shares = [pieces] + [exchange(pieces, "dp", k) for k in range(1, lax.axis_size("dp"))]
    shares = jnp.stack(shares)
    other_shares = swap(shares)
    up = after(sent, turned[: 2 * units])
    hidden = hidden_of(rows, up, after(sent, other[: 2 * units]))
    gathered = lax.all_gather(hidden, "zi", axis=0)
    position = jnp.stack([place, lax.axis_index("dp")]).astype(jnp.int32)
    done = outputs_of(position, gathered, shares, other_shares, experts, slots)
    done = done.reshape(experts * line, slots, columns)
    returned = lax.all_to_all(done, HOME, split_axis=0, concat_axis=0, tiled=True)
    returned = returned.reshape(experts, line, batches, capacity, columns).astype(F32)
    mixed = jnp.einsum("mres,ezmsd->mrzd", weighting, returned, precision=lax.Precision.HIGHEST)
    return mixed.astype(BF).reshape(batches, row_count, width)


def solution(mesh):
    fine = Mesh(mesh.devices.reshape(4, 4, 4, 2, 4), ("x", "zb", "zi", "c", "dp"))
    ep = ("x", "zb", "zi", "c")
    by_row = P(None, ("dp",) + ep, None)
    return jax.shard_map(
        on_device,
        mesh=fine,
        in_specs=(by_row, by_row, by_row, P(ep, None, None)),
        out_specs=by_row,
        check_vma=False,
    )
```

```python
import jax
import jax.numpy as jnp
from jax import lax
from jax.experimental import pallas as pl
from jax.experimental.pallas import tpu as pltpu
from jax.sharding import Mesh, PartitionSpec as P

FF = 1536
BF = jnp.bfloat16
F32 = jnp.float32
ROWS_OF = ("x", "zb")
HOME = ("x", "zb", "zi")
ANYWHERE = pl.BlockSpec(memory_space=pl.ANY)
NT = (((1,), (1,)), ((), ()))


def exchange(array, axis, step):
    size = lax.axis_size(axis)
    return lax.ppermute(array, axis, [(i, i ^ step) for i in range(size)])


def after(first, then):
    mark = first[(0,) * first.ndim]
    return jnp.where(mark == mark, then, jnp.zeros((), then.dtype))


def swap(array):
    return lax.ppermute(array, "c", [(0, 1), (1, 0)])


def pack_kernel(ids_ref, tokens_ref, out_ref):
    batches, picks, rows = ids_ref.shape
    experts, slots, width = out_ref.shape
    capacity = slots // batches
    count = experts * slots
    expert = lax.broadcasted_iota(jnp.int32, (experts, rows), 0)
    row = lax.broadcasted_iota(jnp.int32, (rows, rows), 0)
    earlier = (row < lax.broadcasted_iota(jnp.int32, (rows, rows), 1)).astype(F32)
    owner = lax.broadcasted_iota(jnp.int32, (count, experts), 0) // slots
    spread = (owner == lax.broadcasted_iota(jnp.int32, (count, experts), 1)).astype(F32)
    slot = lax.broadcasted_iota(jnp.int32, (count, rows), 0) % slots
    total = jnp.zeros((count, width), F32)
    for m in range(batches):
        ids = ids_ref[m]
        named = jnp.zeros((experts, rows), jnp.bool_)
        for k in range(picks):
            named = named | (ids[k : k + 1] == expert)
        named = named.astype(F32)
        before = jnp.dot(named, earlier, preferred_element_type=F32)
        named = jnp.dot(spread, named, preferred_element_type=F32)
        before = jnp.dot(spread, before, preferred_element_type=F32)
        here = (slot // capacity == m) & (before == (slot % capacity).astype(F32))
        pick = ((named > 0.5) & here).astype(BF)
        total += jnp.dot(pick, tokens_ref[m], preferred_element_type=F32)
    out_ref[...] = total.astype(BF).reshape(out_ref.shape)


def whole(count):
    return [pl.BlockSpec(memory_space=pltpu.VMEM)] * count


def packed_of(expert_ids, tokens, experts, slots):
    return pl.pallas_call(
        pack_kernel,
        in_specs=whole(2),
        out_specs=whole(1)[0],
        out_shape=jax.ShapeDtypeStruct((experts, slots, tokens.shape[2]), BF),
        compiler_params=pltpu.CompilerParams(vmem_limit_bytes=16 << 20),
    )(expert_ids.transpose(0, 2, 1), tokens)


def repeat_kernel(rows_ref, *refs):
    for k in range(refs[-1].shape[0]):
        refs[-1][k] = rows_ref[...]


def repeat_after(earlier, rows, times):
    return pl.pallas_call(
        repeat_kernel,
        in_specs=whole(1) + [ANYWHERE] * len(earlier),
        out_specs=whole(1)[0],
        out_shape=jax.ShapeDtypeStruct((times,) + rows.shape, rows.dtype),
        compiler_params=pltpu.CompilerParams(vmem_limit_bytes=16 << 20),
    )(rows, *earlier)


def stack_kernel(_, *refs):
    for k, ref in enumerate(refs[:-1]):
        refs[-1][k] = ref[...]


def stack_after(earlier, arrays):
    return pl.pallas_call(
        stack_kernel,
        in_specs=[ANYWHERE] + whole(len(arrays)),
        out_specs=whole(1)[0],
        out_shape=jax.ShapeDtypeStruct((len(arrays),) + arrays[0].shape, arrays[0].dtype),
        compiler_params=pltpu.CompilerParams(vmem_limit_bytes=16 << 20),
    )(earlier, *arrays)


def up_kernel(rows_ref, own_ref, other_ref, out_ref):
    units = own_ref.shape[0] // 2
    rows = rows_ref[...].reshape(-1, own_ref.shape[1])
    hidden = []
    for ref in (own_ref, other_ref):
        both = lax.dot_general(ref[...], rows, NT, preferred_element_type=F32)
        gate = both[:units]
        hidden.append(gate / (1.0 + jnp.exp(-gate)) * both[units:])
    out_ref[...] = jnp.concatenate(hidden, axis=0).T.astype(BF)


def hidden_of(rows, own, other):
    count = rows.shape[0] * rows.shape[1]
    return pl.pallas_call(
        up_kernel,
        grid=(1,),
        in_specs=whole(2) + [pl.BlockSpec(own.shape, lambda i: (0, 0))],
        out_specs=whole(1)[0],
        out_shape=jax.ShapeDtypeStruct((count, own.shape[0]), BF),
        compiler_params=pltpu.CompilerParams(vmem_limit_bytes=48 << 20),
    )(rows, own, other)


def down_kernel(place_ref, hidden_ref, own_ref, other_ref, out_ref):
    shares, line = own_ref.shape[:2]
    experts, _, slots, columns = out_ref.shape
    total = jnp.zeros((line * experts * slots, columns), F32)
    for at in range(line):
        k = place_ref[0] ^ at
        weights = [ref[place_ref[1] ^ y, k] for ref in (own_ref, other_ref) for y in range(shares)]
        weights = jnp.concatenate(weights, axis=0)
        total += jnp.dot(hidden_ref[at], weights, preferred_element_type=F32)
    total = total.astype(BF).reshape(line, experts, slots, columns)
    for p in range(line):
        out_ref[:, p] = total[p]


def outputs_of(place, hidden, own, other, experts, slots):
    return pl.pallas_call(
        down_kernel,
        in_specs=[pl.BlockSpec(memory_space=pltpu.SMEM)] + whole(3),
        out_specs=whole(1)[0],
        out_shape=jax.ShapeDtypeStruct((experts, hidden.shape[0], slots, own.shape[3]), BF),
        compiler_params=pltpu.CompilerParams(vmem_limit_bytes=16 << 20),
    )(place, hidden, own, other)


def on_device(tokens, expert_ids, gate_scores, expert_weights):
    batches, row_count, width = tokens.shape
    experts = lax.axis_size("x") * lax.axis_size("zb")
    line = lax.axis_size("zi")
    capacity = 2
    slots = batches * capacity
    columns = width // line
    turned = expert_weights[0].T
    units = turned.shape[0] // 3
    place = lax.axis_index("zi")
    share = units // lax.axis_size("dp")
    down = lax.dynamic_slice_in_dim(turned, 2 * units + share * lax.axis_index("dp"), share, 0)
    down = down.reshape(share, line, columns)

    def for_place(at):
        return lax.dynamic_index_in_dim(down, at, 1, keepdims=False)

    pieces = [for_place(place)] + [exchange(for_place(place ^ k), "zi", k) for k in range(1, line)]
    other = swap(turned)

    matches = (expert_ids[..., None] == jnp.arange(experts, dtype=jnp.int32)).astype(jnp.int32)
    present = jnp.sum(matches, axis=2)
    before = jnp.cumsum(present, axis=1) - present
    occurrence = jnp.sum(matches * before[:, :, None, :], axis=3)
    slot = jnp.arange(capacity, dtype=jnp.int32)
    landing = (
        (expert_ids[..., None, None] == jnp.arange(experts, dtype=jnp.int32)[:, None])
        & (occurrence[..., None, None] == slot)
    ).astype(F32)
    weighting = jnp.sum(landing * gate_scores[..., None, None], axis=2)
    packed = packed_of(expert_ids, tokens, experts, slots)
    arrived = lax.all_to_all(packed, ROWS_OF, split_axis=0, concat_axis=0, tiled=True)
    sent = repeat_after(pieces[1:], arrived, line)
    rows = lax.all_to_all(sent, "zi", split_axis=0, concat_axis=0, tiled=True)
    rows = rows.reshape(line * experts, slots, width)
    pieces = stack_after(sent, pieces)
    shares = [pieces] + [exchange(pieces, "dp", k) for k in range(1, lax.axis_size("dp"))]
    shares = jnp.stack(shares)
    other_shares = swap(shares)
    up = after(sent, turned[: 2 * units])
    hidden = hidden_of(rows, up, other)
    gathered = lax.all_gather(hidden, "zi", axis=0)
    position = jnp.stack([place, lax.axis_index("dp")]).astype(jnp.int32)
    done = outputs_of(position, gathered, shares, other_shares, experts, slots)
    done = done.reshape(experts * line, slots, columns)
    returned = lax.all_to_all(done, HOME, split_axis=0, concat_axis=0, tiled=True)
    returned = returned.reshape(experts, line, batches, capacity, columns).astype(F32)
    mixed = jnp.einsum("mres,ezmsd->mrzd", weighting, returned, precision=lax.Precision.HIGHEST)
    return mixed.astype(BF).reshape(batches, row_count, width)


def solution(mesh):
    fine = Mesh(mesh.devices.reshape(4, 4, 4, 2, 4), ("x", "zb", "zi", "c", "dp"))
    ep = ("x", "zb", "zi", "c")
    by_row = P(None, ("dp",) + ep, None)
    return jax.shard_map(
        on_device,
        mesh=fine,
        in_specs=(by_row, by_row, by_row, P(ep, None, None)),
        out_specs=by_row,
        check_vma=False,
    )
```

```python
import jax
import jax.numpy as jnp
from jax import lax
from jax.experimental import pallas as pl
from jax.experimental.pallas import tpu as pltpu
from jax.sharding import Mesh, PartitionSpec as P

FF = 1536
BF = jnp.bfloat16
F32 = jnp.float32
ROWS_OF = ("x", "zb")
HOME = ("x", "zb", "zi")
ANYWHERE = pl.BlockSpec(memory_space=pl.ANY)
NT = (((1,), (1,)), ((), ()))


def exchange(array, axis, step):
    size = lax.axis_size(axis)
    return lax.ppermute(array, axis, [(i, i ^ step) for i in range(size)])


def swap(array):
    return lax.ppermute(array, "c", [(0, 1), (1, 0)])


def pack_kernel(ids_ref, gates_ref, tokens_ref, out_ref, weights_ref):
    batches, picks, rows = ids_ref.shape
    experts, slots, width = out_ref.shape
    capacity = slots // batches
    count = experts * slots
    expert = lax.broadcasted_iota(jnp.int32, (experts, rows), 0)
    row = lax.broadcasted_iota(jnp.int32, (rows, rows), 0)
    earlier = (row < lax.broadcasted_iota(jnp.int32, (rows, rows), 1)).astype(F32)
    owner = lax.broadcasted_iota(jnp.int32, (count, experts), 0) // slots
    spread = (owner == lax.broadcasted_iota(jnp.int32, (count, experts), 1)).astype(F32)
    slot = lax.broadcasted_iota(jnp.int32, (count, rows), 0) % slots
    total = jnp.zeros((count, width), F32)
    for m in range(batches):
        ids, gates = ids_ref[m], gates_ref[m]
        named = jnp.zeros((experts, rows), jnp.bool_)
        weight = jnp.zeros((experts, rows), F32)
        for k in range(picks):
            hit = ids[k : k + 1] == expert
            named = named | hit
            weight = jnp.where(hit, gates[k : k + 1], weight)
        named = named.astype(F32)
        before = jnp.dot(named, earlier, preferred_element_type=F32)
        for s in range(capacity):
            weights_ref[m, s] = jnp.where(before == s, weight, 0.0)
        named = jnp.dot(spread, named, preferred_element_type=F32)
        before = jnp.dot(spread, before, preferred_element_type=F32)
        here = (slot // capacity == m) & (before == (slot % capacity).astype(F32))
        pick = ((named > 0.5) & here).astype(BF)
        total += jnp.dot(pick, tokens_ref[m], preferred_element_type=F32)
    out_ref[...] = total.astype(BF).reshape(out_ref.shape)


def whole(count):
    return [pl.BlockSpec(memory_space=pltpu.VMEM)] * count


def packed_of(expert_ids, gate_scores, tokens, experts, slots):
    batches, rows, width = tokens.shape
    return pl.pallas_call(
        pack_kernel,
        in_specs=whole(3),
        out_specs=whole(2),
        out_shape=[
            jax.ShapeDtypeStruct((experts, slots, width), BF),
            jax.ShapeDtypeStruct((batches, slots // batches, experts, rows), F32),
        ],
        compiler_params=pltpu.CompilerParams(vmem_limit_bytes=16 << 20),
    )(expert_ids.transpose(0, 2, 1), gate_scores.transpose(0, 2, 1), tokens)


def repeat_kernel(_, *refs):
    arrays, out_ref, done = refs[:-2], refs[-2], refs[-1]
    copies = [
        pltpu.make_async_copy(ref, out_ref.at[copy, k], done.at[copy, k])
        for copy in range(out_ref.shape[0])
        for k, ref in enumerate(arrays)
    ]
    for copy in copies:
        copy.start()
    for copy in copies:
        copy.wait()


def repeat_after(earlier, arrays, times):
    return pl.pallas_call(
        repeat_kernel,
        in_specs=[ANYWHERE] + whole(len(arrays)),
        out_specs=pl.BlockSpec(memory_space=pltpu.HBM),
        out_shape=jax.ShapeDtypeStruct((times, len(arrays)) + arrays[0].shape, BF),
        scratch_shapes=[pltpu.SemaphoreType.DMA((times, len(arrays)))],
        compiler_params=pltpu.CompilerParams(vmem_limit_bytes=53 << 20),
    )(earlier, *arrays)


def copy_kernel(_, array_ref, out_ref):
    out_ref[...] = array_ref[...]


def copy_after(earlier, array):
    return pl.pallas_call(
        copy_kernel,
        in_specs=[ANYWHERE] + whole(1),
        out_specs=whole(1)[0],
        out_shape=jax.ShapeDtypeStruct(array.shape, array.dtype),
        compiler_params=pltpu.CompilerParams(vmem_limit_bytes=16 << 20),
    )(earlier, array)


def up_kernel(first_ref, second_ref, own_ref, other_ref, out_ref):
    units = own_ref.shape[0] // 3
    width = own_ref.shape[1]
    rows = [ref[...].reshape(-1, width) for ref in (first_ref, second_ref)]
    rows = jnp.concatenate(rows, axis=0)
    hidden = []
    for ref in (own_ref, other_ref):
        both = lax.dot_general(ref[: 2 * units], rows, NT, preferred_element_type=F32)
        gate = both[:units]
        hidden.append(gate / (1.0 + jnp.exp(-gate)) * both[units:])
    out_ref[...] = jnp.concatenate(hidden, axis=0).T.astype(BF)


def hidden_of(first, second, own, other):
    count = 2 * first.shape[0] * first.shape[1]
    both = own.shape[0] // 3 * 2
    return pl.pallas_call(
        up_kernel,
        grid=(1,),
        in_specs=whole(3) + [pl.BlockSpec((both, own.shape[1]), lambda i: (0, 0))],
        out_specs=whole(1)[0],
        out_shape=jax.ShapeDtypeStruct((count, both), BF),
        compiler_params=pltpu.CompilerParams(vmem_limit_bytes=24 << 20),
    )(first, second, own, other)


def down_kernel(place_ref, hidden_ref, own_ref, other_ref, out_ref):
    shares, line = own_ref.shape[:2]
    experts, _, slots, columns = out_ref.shape
    total = jnp.zeros((line * experts * slots, columns), F32)
    for at in range(line):
        k = place_ref[0] ^ at
        weights = [ref[y, k] for ref in (own_ref, other_ref) for y in range(shares)]
        weights = jnp.concatenate(weights, axis=0)
        total += jnp.dot(hidden_ref[at], weights, preferred_element_type=F32)
    half = experts // 2
    total = total.astype(BF).reshape(2, line, half, slots, columns)
    for part in range(2):
        for p in range(line):
            out_ref[part * half : (part + 1) * half, p] = total[part, p]


def outputs_of(place, hidden, own, other, experts, slots):
    return pl.pallas_call(
        down_kernel,
        in_specs=[pl.BlockSpec(memory_space=pltpu.SMEM)] + whole(3),
        out_specs=whole(1)[0],
        out_shape=jax.ShapeDtypeStruct((experts, hidden.shape[0], slots, own.shape[3]), BF),
        compiler_params=pltpu.CompilerParams(vmem_limit_bytes=16 << 20),
    )(place, hidden, own, other)


def on_device(tokens, expert_ids, gate_scores, expert_weights):
    batches, row_count, width = tokens.shape
    experts = lax.axis_size("x") * lax.axis_size("zb")
    line = lax.axis_size("zi")
    capacity = 2
    slots = batches * capacity
    columns = width // line
    turned = expert_weights[0].T
    units = turned.shape[0] // 3
    place = lax.axis_index("zi")
    share = units // lax.axis_size("dp")
    down = lax.dynamic_slice_in_dim(turned, 2 * units + share * lax.axis_index("dp"), share, 0)
    down = down.reshape(share, line, columns)

    def for_place(at):
        return lax.dynamic_index_in_dim(down, at, 1, keepdims=False)

    pieces = [for_place(place)] + [exchange(for_place(place ^ k), "zi", k) for k in range(1, line)]
    packed, weighting = packed_of(expert_ids, gate_scores, tokens, experts, slots)
    mark = weighting[0, 0, 0, 0]
    other = swap(jnp.where(mark == mark, turned[: 2 * units], jnp.zeros((), BF)))
    arrived = lax.all_to_all(packed, ROWS_OF, split_axis=0, concat_axis=0, tiled=True)
    shares = repeat_after(arrived, pieces, lax.axis_size("dp"))
    shares = lax.all_to_all(shares, "dp", split_axis=0, concat_axis=0, tiled=True)
    half = experts // 2
    first = lax.all_gather(arrived[:half], "zi", axis=0, tiled=True)
    second = lax.all_gather(arrived[half:], "zi", axis=0, tiled=True)
    shares = copy_after(second, shares)
    other_shares = swap(shares)
    hidden = hidden_of(first, second, turned, other)
    gathered = lax.all_gather(hidden, "zi", axis=0)
    position = place.astype(jnp.int32).reshape(1)
    done = outputs_of(position, gathered, shares, other_shares, experts, slots)
    done = done.reshape(experts * line, slots, columns)
    returned = lax.all_to_all(done, HOME, split_axis=0, concat_axis=0, tiled=True)
    returned = returned.reshape(experts, line, batches, capacity, columns).astype(F32)
    mixed = jnp.einsum("mser,ezmsd->mrzd", weighting, returned, precision=lax.Precision.HIGHEST)
    return mixed.astype(BF).reshape(batches, row_count, width)


def solution(mesh):
    fine = Mesh(mesh.devices.reshape(4, 4, 4, 2, 4), ("x", "zb", "zi", "c", "dp"))
    ep = ("x", "zb", "zi", "c")
    by_row = P(None, ("dp",) + ep, None)
    return jax.shard_map(
        on_device,
        mesh=fine,
        in_specs=(by_row, by_row, by_row, P(ep, None, None)),
        out_specs=by_row,
        check_vma=False,
    )
```

```python
import jax
import jax.numpy as jnp
from jax import lax
from jax.experimental import pallas as pl
from jax.experimental.pallas import tpu as pltpu
from jax.sharding import Mesh, PartitionSpec as P

FF = 1536
BF = jnp.bfloat16
F32 = jnp.float32
ROWS_OF = ("x", "zb")
HOME = ("x", "zb", "zi")
ANYWHERE = pl.BlockSpec(memory_space=pl.ANY)
NT = (((1,), (1,)), ((), ()))


def exchange(array, axis, step):
    size = lax.axis_size(axis)
    return lax.ppermute(array, axis, [(i, i ^ step) for i in range(size)])


def swap(array):
    return lax.ppermute(array, "c", [(0, 1), (1, 0)])


def pack_kernel(ids_ref, gates_ref, tokens_ref, out_ref, weights_ref):
    batches, picks, rows = ids_ref.shape
    experts, slots, width = out_ref.shape
    capacity = slots // batches
    count = experts * slots
    expert = lax.broadcasted_iota(jnp.int32, (experts, rows), 0)
    row = lax.broadcasted_iota(jnp.int32, (rows, rows), 0)
    earlier = (row < lax.broadcasted_iota(jnp.int32, (rows, rows), 1)).astype(F32)
    owner = lax.broadcasted_iota(jnp.int32, (count, experts), 0) // slots
    spread = (owner == lax.broadcasted_iota(jnp.int32, (count, experts), 1)).astype(F32)
    slot = lax.broadcasted_iota(jnp.int32, (count, rows), 0) % slots
    total = jnp.zeros((count, width), F32)
    for m in range(batches):
        ids, gates = ids_ref[m], gates_ref[m]
        named = jnp.zeros((experts, rows), jnp.bool_)
        weight = jnp.zeros((experts, rows), F32)
        for k in range(picks):
            hit = ids[k : k + 1] == expert
            named = named | hit
            weight = jnp.where(hit, gates[k : k + 1], weight)
        named = named.astype(F32)
        before = jnp.dot(named, earlier, preferred_element_type=F32)
        for s in range(capacity):
            weights_ref[m, s] = jnp.where(before == s, weight, 0.0)
        named = jnp.dot(spread, named, preferred_element_type=F32)
        before = jnp.dot(spread, before, preferred_element_type=F32)
        here = (slot // capacity == m) & (before == (slot % capacity).astype(F32))
        pick = ((named > 0.5) & here).astype(BF)
        total += jnp.dot(pick, tokens_ref[m], preferred_element_type=F32)
    out_ref[...] = total.astype(BF).reshape(out_ref.shape)


def whole(count):
    return [pl.BlockSpec(memory_space=pltpu.VMEM)] * count


def packed_of(expert_ids, gate_scores, tokens, experts, slots):
    batches, rows, width = tokens.shape
    return pl.pallas_call(
        pack_kernel,
        in_specs=whole(3),
        out_specs=whole(2),
        out_shape=[
            jax.ShapeDtypeStruct((experts, slots, width), BF),
            jax.ShapeDtypeStruct((batches, slots // batches, experts, rows), F32),
        ],
        compiler_params=pltpu.CompilerParams(vmem_limit_bytes=16 << 20),
    )(expert_ids.transpose(0, 2, 1), gate_scores.transpose(0, 2, 1), tokens)


def repeat_kernel(_, __, *refs):
    arrays, out_ref, done = refs[:-2], refs[-2], refs[-1]
    copies = [
        pltpu.make_async_copy(ref, out_ref.at[copy, k], done.at[copy, k])
        for copy in range(out_ref.shape[0])
        for k, ref in enumerate(arrays)
    ]
    for copy in copies:
        copy.start()
    for copy in copies:
        copy.wait()


def repeat_after(earlier, arrays, times):
    return pl.pallas_call(
        repeat_kernel,
        in_specs=[ANYWHERE] * 2 + whole(len(arrays)),
        out_specs=pl.BlockSpec(memory_space=pltpu.HBM),
        out_shape=jax.ShapeDtypeStruct((times, len(arrays)) + arrays[0].shape, BF),
        scratch_shapes=[pltpu.SemaphoreType.DMA((times, len(arrays)))],
        compiler_params=pltpu.CompilerParams(vmem_limit_bytes=50 << 20),
    )(*earlier, *arrays)


def up_kernel(first_ref, second_ref, own_ref, other_ref, out_ref):
    units = own_ref.shape[0] // 2
    width = own_ref.shape[1]
    rows = [ref[...].reshape(-1, width) for ref in (first_ref, second_ref)]
    rows = jnp.concatenate(rows, axis=0)
    hidden = []
    for ref in (own_ref, other_ref):
        both = lax.dot_general(ref[: 2 * units], rows, NT, preferred_element_type=F32)
        gate = both[:units]
        hidden.append(gate / (1.0 + jnp.exp(-gate)) * both[units:])
    out_ref[...] = jnp.concatenate(hidden, axis=0).T.astype(BF)


def hidden_of(first, second, own, other):
    count = 2 * first.shape[0] * first.shape[1]
    both = own.shape[0]
    return pl.pallas_call(
        up_kernel,
        grid=(1,),
        in_specs=whole(3) + [pl.BlockSpec((both, own.shape[1]), lambda i: (0, 0))],
        out_specs=whole(1)[0],
        out_shape=jax.ShapeDtypeStruct((count, both), BF),
        compiler_params=pltpu.CompilerParams(vmem_limit_bytes=24 << 20),
    )(first, second, own, other)


def down_kernel(place_ref, hidden_ref, shares_ref, out_ref):
    shares, cores, line = shares_ref.shape[:3]
    experts, _, slots, columns = out_ref.shape
    total = jnp.zeros((line * experts * slots, columns), F32)
    for at in range(line):
        k = place_ref[0] ^ at
        weights = [
            shares_ref[y, place_ref[1] ^ core, k] for core in range(cores) for y in range(shares)
        ]
        weights = jnp.concatenate(weights, axis=0)
        total += jnp.dot(hidden_ref[at], weights, preferred_element_type=F32)
    half = experts // 2
    total = total.astype(BF).reshape(2, line, half, slots, columns)
    for part in range(2):
        for p in range(line):
            out_ref[part * half : (part + 1) * half, p] = total[part, p]


def outputs_of(place, hidden, shares, experts, slots):
    return pl.pallas_call(
        down_kernel,
        in_specs=[pl.BlockSpec(memory_space=pltpu.SMEM)] + whole(2),
        out_specs=whole(1)[0],
        out_shape=jax.ShapeDtypeStruct((experts, hidden.shape[0], slots, shares.shape[-1]), BF),
        compiler_params=pltpu.CompilerParams(vmem_limit_bytes=16 << 20),
    )(place, hidden, shares)


def on_device(tokens, expert_ids, gate_scores, expert_weights):
    batches, row_count, width = tokens.shape
    experts = lax.axis_size("x") * lax.axis_size("zb")
    line = lax.axis_size("zi")
    capacity = 2
    slots = batches * capacity
    columns = width // line
    turned = expert_weights[0].T
    units = turned.shape[0] // 3
    place = lax.axis_index("zi")
    share = units // lax.axis_size("dp")
    down = lax.dynamic_slice_in_dim(turned, 2 * units + share * lax.axis_index("dp"), share, 0)
    down = down.reshape(share, line, columns)

    def for_place(at):
        return lax.dynamic_index_in_dim(down, at, 1, keepdims=False)

    other = swap(turned)
    pieces = [for_place(place)] + [exchange(for_place(place ^ k), "zi", k) for k in range(1, line)]
    packed, weighting = packed_of(expert_ids, gate_scores, tokens, experts, slots)
    arrived = lax.all_to_all(packed, ROWS_OF, split_axis=0, concat_axis=0, tiled=True)
    mark = pieces[1][0, 0]
    up = jnp.where(mark == mark, turned[: 2 * units], jnp.zeros((), BF))
    replicas, cores = lax.axis_size("dp"), lax.axis_size("c")
    shares = repeat_after((arrived, up), pieces, replicas * cores)
    shares = lax.all_to_all(shares, ("dp", "c"), split_axis=0, concat_axis=0, tiled=True)
    shares = shares.reshape((replicas, cores) + shares.shape[1:])
    half = experts // 2
    first = lax.all_gather(arrived[:half], "zi", axis=0, tiled=True)
    second = lax.all_gather(arrived[half:], "zi", axis=0, tiled=True)
    hidden = hidden_of(first, second, up, other)
    gathered = lax.all_gather(hidden, "zi", axis=0)
    position = jnp.stack([place, lax.axis_index("c")]).astype(jnp.int32)
    done = outputs_of(position, gathered, shares, experts, slots)
    done = done.reshape(experts * line, slots, columns)
    returned = lax.all_to_all(done, HOME, split_axis=0, concat_axis=0, tiled=True)
    returned = returned.reshape(experts, line, batches, capacity, columns).astype(F32)
    mixed = jnp.einsum("mser,ezmsd->mrzd", weighting, returned, precision=lax.Precision.HIGHEST)
    return mixed.astype(BF).reshape(batches, row_count, width)


def solution(mesh):
    fine = Mesh(mesh.devices.reshape(4, 4, 4, 2, 4), ("x", "zb", "zi", "c", "dp"))
    ep = ("x", "zb", "zi", "c")
    by_row = P(None, ("dp",) + ep, None)
    return jax.shard_map(
        on_device,
        mesh=fine,
        in_specs=(by_row, by_row, by_row, P(ep, None, None)),
        out_specs=by_row,
        check_vma=False,
    )
```

```python
import jax
import jax.numpy as jnp
from jax import lax
from jax.experimental import pallas as pl
from jax.experimental.pallas import tpu as pltpu
from jax.sharding import Mesh, PartitionSpec as P

FF = 1536
BF = jnp.bfloat16
F32 = jnp.float32
ROWS_OF = ("x", "zb")
HOME = ("x", "zb", "zi")
ANYWHERE = pl.BlockSpec(memory_space=pl.ANY)
NT = (((1,), (1,)), ((), ()))


def exchange(array, axis, step):
    size = lax.axis_size(axis)
    return lax.ppermute(array, axis, [(i, i ^ step) for i in range(size)])


def swap(array):
    return lax.ppermute(array, "c", [(0, 1), (1, 0)])


def pack_kernel(ids_ref, gates_ref, tokens_ref, out_ref, weights_ref):
    batches, picks, rows = ids_ref.shape
    experts, slots, width = out_ref.shape
    capacity = slots // batches
    count = experts * slots
    expert = lax.broadcasted_iota(jnp.int32, (experts, rows), 0)
    row = lax.broadcasted_iota(jnp.int32, (rows, rows), 0)
    earlier = (row < lax.broadcasted_iota(jnp.int32, (rows, rows), 1)).astype(F32)
    owner = lax.broadcasted_iota(jnp.int32, (count, experts), 0) // slots
    spread = (owner == lax.broadcasted_iota(jnp.int32, (count, experts), 1)).astype(F32)
    slot = lax.broadcasted_iota(jnp.int32, (count, rows), 0) % slots
    total = jnp.zeros((count, width), F32)
    for m in range(batches):
        ids, gates = ids_ref[m], gates_ref[m]
        named = jnp.zeros((experts, rows), jnp.bool_)
        weight = jnp.zeros((experts, rows), F32)
        for k in range(picks):
            hit = ids[k : k + 1] == expert
            named = named | hit
            weight = jnp.where(hit, gates[k : k + 1], weight)
        named = named.astype(F32)
        before = jnp.dot(named, earlier, preferred_element_type=F32)
        for s in range(capacity):
            weights_ref[m, s] = jnp.where(before == s, weight, 0.0)
        named = jnp.dot(spread, named, preferred_element_type=F32)
        before = jnp.dot(spread, before, preferred_element_type=F32)
        here = (slot // capacity == m) & (before == (slot % capacity).astype(F32))
        pick = ((named > 0.5) & here).astype(BF)
        total += jnp.dot(pick, tokens_ref[m], preferred_element_type=F32)
    out_ref[...] = total.astype(BF).reshape(out_ref.shape)


def whole(count):
    return [pl.BlockSpec(memory_space=pltpu.VMEM)] * count


def packed_of(expert_ids, gate_scores, tokens, experts, slots):
    batches, rows, width = tokens.shape
    return pl.pallas_call(
        pack_kernel,
        in_specs=whole(3),
        out_specs=whole(2),
        out_shape=[
            jax.ShapeDtypeStruct((experts, slots, width), BF),
            jax.ShapeDtypeStruct((batches, slots // batches, experts, rows), F32),
        ],
        compiler_params=pltpu.CompilerParams(vmem_limit_bytes=16 << 20),
    )(expert_ids.transpose(0, 2, 1), gate_scores.transpose(0, 2, 1), tokens)


def repeat_kernel(_, *refs):
    arrays, out_ref, done = refs[:-2], refs[-2], refs[-1]
    copies = [
        pltpu.make_async_copy(ref, out_ref.at[copy, k], done.at[copy, k])
        for copy in range(out_ref.shape[0])
        for k, ref in enumerate(arrays)
    ]
    for copy in copies:
        copy.start()
    for copy in copies:
        copy.wait()


def repeat_after(earlier, arrays, times):
    return pl.pallas_call(
        repeat_kernel,
        in_specs=[ANYWHERE] + whole(len(arrays)),
        out_specs=pl.BlockSpec(memory_space=pltpu.HBM),
        out_shape=jax.ShapeDtypeStruct((times, len(arrays)) + arrays[0].shape, BF),
        scratch_shapes=[pltpu.SemaphoreType.DMA((times, len(arrays)))],
        compiler_params=pltpu.CompilerParams(vmem_limit_bytes=53 << 20),
    )(earlier, *arrays)


def up_kernel(first_ref, second_ref, own_ref, other_ref, out_ref):
    units = own_ref.shape[0] // 2
    width = own_ref.shape[1]
    rows = [ref[...].reshape(-1, width) for ref in (first_ref, second_ref)]
    rows = jnp.concatenate(rows, axis=0)
    hidden = []
    for ref in (own_ref, other_ref):
        both = lax.dot_general(ref[: 2 * units], rows, NT, preferred_element_type=F32)
        gate = both[:units]
        hidden.append(gate / (1.0 + jnp.exp(-gate)) * both[units:])
    out_ref[...] = jnp.concatenate(hidden, axis=0).T.astype(BF)


def hidden_of(first, second, own, other):
    count = 2 * first.shape[0] * first.shape[1]
    both = own.shape[0]
    return pl.pallas_call(
        up_kernel,
        grid=(1,),
        in_specs=whole(3) + [pl.BlockSpec((both, own.shape[1]), lambda i: (0, 0))],
        out_specs=whole(1)[0],
        out_shape=jax.ShapeDtypeStruct((count, both), BF),
        compiler_params=pltpu.CompilerParams(vmem_limit_bytes=24 << 20),
    )(first, second, own, other)


def down_kernel(place_ref, hidden_ref, shares_ref, out_ref):
    shares, cores, line = shares_ref.shape[:3]
    experts, _, slots, columns = out_ref.shape
    total = jnp.zeros((line * experts * slots, columns), F32)
    for at in range(line):
        k = place_ref[0] ^ at
        weights = [
            shares_ref[y, place_ref[1] ^ core, k] for core in range(cores) for y in range(shares)
        ]
        weights = jnp.concatenate(weights, axis=0)
        total += jnp.dot(hidden_ref[at], weights, preferred_element_type=F32)
    half = experts // 2
    total = total.astype(BF).reshape(2, line, half, slots, columns)
    for part in range(2):
        for p in range(line):
            out_ref[part * half : (part + 1) * half, p] = total[part, p]


def outputs_of(place, hidden, shares, experts, slots):
    return pl.pallas_call(
        down_kernel,
        in_specs=[pl.BlockSpec(memory_space=pltpu.SMEM)] + whole(2),
        out_specs=whole(1)[0],
        out_shape=jax.ShapeDtypeStruct((experts, hidden.shape[0], slots, shares.shape[-1]), BF),
        compiler_params=pltpu.CompilerParams(vmem_limit_bytes=16 << 20),
    )(place, hidden, shares)


def on_device(tokens, expert_ids, gate_scores, expert_weights):
    batches, row_count, width = tokens.shape
    experts = lax.axis_size("x") * lax.axis_size("zb")
    line = lax.axis_size("zi")
    capacity = 2
    slots = batches * capacity
    columns = width // line
    turned = expert_weights[0].T
    units = turned.shape[0] // 3
    place = lax.axis_index("zi")
    share = units // lax.axis_size("dp")
    down = lax.dynamic_slice_in_dim(turned, 2 * units + share * lax.axis_index("dp"), share, 0)
    down = down.reshape(share, line, columns)

    def for_place(at):
        return lax.dynamic_index_in_dim(down, at, 1, keepdims=False)

    pieces = [for_place(place)] + [exchange(for_place(place ^ k), "zi", k) for k in range(1, line)]
    packed, weighting = packed_of(expert_ids, gate_scores, tokens, experts, slots)
    mark = weighting[0, 0, 0, 0]
    up = jnp.where(mark == mark, turned[: 2 * units], jnp.zeros((), BF))
    other = swap(up)
    arrived = lax.all_to_all(packed, ROWS_OF, split_axis=0, concat_axis=0, tiled=True)
    replicas, cores = lax.axis_size("dp"), lax.axis_size("c")
    shares = repeat_after(arrived, pieces, replicas * cores)
    shares = lax.all_to_all(shares, ("dp", "c"), split_axis=0, concat_axis=0, tiled=True)
    shares = shares.reshape((replicas, cores) + shares.shape[1:])
    half = experts // 2
    first = lax.all_gather(arrived[:half], "zi", axis=0, tiled=True)
    second = lax.all_gather(arrived[half:], "zi", axis=0, tiled=True)
    hidden = hidden_of(first, second, up, other)
    gathered = lax.all_gather(hidden, "zi", axis=0)
    position = jnp.stack([place, lax.axis_index("c")]).astype(jnp.int32)
    done = outputs_of(position, gathered, shares, experts, slots)
    done = done.reshape(experts * line, slots, columns)
    returned = lax.all_to_all(done, HOME, split_axis=0, concat_axis=0, tiled=True)
    returned = returned.reshape(experts, line, batches, capacity, columns).astype(F32)
    mixed = jnp.einsum("mser,ezmsd->mrzd", weighting, returned, precision=lax.Precision.HIGHEST)
    return mixed.astype(BF).reshape(batches, row_count, width)


def solution(mesh):
    fine = Mesh(mesh.devices.reshape(4, 4, 4, 2, 4), ("x", "zb", "zi", "c", "dp"))
    ep = ("x", "zb", "zi", "c")
    by_row = P(None, ("dp",) + ep, None)
    return jax.shard_map(
        on_device,
        mesh=fine,
        in_specs=(by_row, by_row, by_row, P(ep, None, None)),
        out_specs=by_row,
        check_vma=False,
    )
```

```python
import jax
import jax.numpy as jnp
from jax import lax
from jax.experimental import pallas as pl
from jax.experimental.pallas import tpu as pltpu
from jax.sharding import Mesh, PartitionSpec as P

FF = 1536
BF = jnp.bfloat16
F32 = jnp.float32
ROWS_OF = ("x", "zb")
HOME = ("x", "zb", "zi")
ANYWHERE = pl.BlockSpec(memory_space=pl.ANY)
NT = (((1,), (1,)), ((), ()))


def exchange(array, axis, step):
    size = lax.axis_size(axis)
    return lax.ppermute(array, axis, [(i, i ^ step) for i in range(size)])


def swap(array):
    return lax.ppermute(array, "c", [(0, 1), (1, 0)])


def pack_kernel(ids_ref, gates_ref, tokens_ref, out_ref, weights_ref):
    batches, picks, rows = ids_ref.shape
    experts, slots, width = out_ref.shape
    capacity = slots // batches
    count = experts * slots
    expert = lax.broadcasted_iota(jnp.int32, (experts, rows), 0)
    row = lax.broadcasted_iota(jnp.int32, (rows, rows), 0)
    earlier = (row < lax.broadcasted_iota(jnp.int32, (rows, rows), 1)).astype(F32)
    owner = lax.broadcasted_iota(jnp.int32, (count, experts), 0) // slots
    spread = (owner == lax.broadcasted_iota(jnp.int32, (count, experts), 1)).astype(F32)
    slot = lax.broadcasted_iota(jnp.int32, (count, rows), 0) % slots
    total = jnp.zeros((count, width), F32)
    for m in range(batches):
        ids, gates = ids_ref[m], gates_ref[m]
        named = jnp.zeros((experts, rows), jnp.bool_)
        weight = jnp.zeros((experts, rows), F32)
        for k in range(picks):
            hit = ids[k : k + 1] == expert
            named = named | hit
            weight = jnp.where(hit, gates[k : k + 1], weight)
        named = named.astype(F32)
        before = jnp.dot(named, earlier, preferred_element_type=F32)
        for s in range(capacity):
            weights_ref[m, s] = jnp.where(before == s, weight, 0.0)
        named = jnp.dot(spread, named, preferred_element_type=F32)
        before = jnp.dot(spread, before, preferred_element_type=F32)
        here = (slot // capacity == m) & (before == (slot % capacity).astype(F32))
        pick = ((named > 0.5) & here).astype(BF)
        total += jnp.dot(pick, tokens_ref[m], preferred_element_type=F32)
    out_ref[...] = total.astype(BF).reshape(out_ref.shape)


def whole(count):
    return [pl.BlockSpec(memory_space=pltpu.VMEM)] * count


def packed_of(expert_ids, gate_scores, tokens, experts, slots):
    batches, rows, width = tokens.shape
    return pl.pallas_call(
        pack_kernel,
        in_specs=whole(3),
        out_specs=whole(2),
        out_shape=[
            jax.ShapeDtypeStruct((experts, slots, width), BF),
            jax.ShapeDtypeStruct((batches, slots // batches, experts, rows), F32),
        ],
        compiler_params=pltpu.CompilerParams(vmem_limit_bytes=16 << 20),
    )(expert_ids.transpose(0, 2, 1), gate_scores.transpose(0, 2, 1), tokens)


def repeat_kernel(_, *refs):
    arrays, out_ref, done = refs[:-2], refs[-2], refs[-1]
    copies = [
        pltpu.make_async_copy(ref, out_ref.at[copy, k], done.at[copy, k])
        for copy in range(out_ref.shape[0])
        for k, ref in enumerate(arrays)
    ]
    for copy in copies:
        copy.start()
    for copy in copies:
        copy.wait()


def repeat_after(earlier, arrays, times):
    return pl.pallas_call(
        repeat_kernel,
        in_specs=[ANYWHERE] + whole(len(arrays)),
        out_specs=pl.BlockSpec(memory_space=pltpu.HBM),
        out_shape=jax.ShapeDtypeStruct((times, len(arrays)) + arrays[0].shape, BF),
        scratch_shapes=[pltpu.SemaphoreType.DMA((times, len(arrays)))],
        compiler_params=pltpu.CompilerParams(vmem_limit_bytes=53 << 20),
    )(earlier, *arrays)


def up_kernel(first_ref, second_ref, own_ref, other_ref, out_ref):
    units = own_ref.shape[0] // 2
    width = own_ref.shape[1]
    rows = [ref[...].reshape(-1, width) for ref in (first_ref, second_ref)]
    rows = jnp.concatenate(rows, axis=0)
    hidden = []
    for ref in (own_ref, other_ref):
        both = lax.dot_general(ref[: 2 * units], rows, NT, preferred_element_type=F32)
        gate = both[:units]
        hidden.append(gate / (1.0 + jnp.exp(-gate)) * both[units:])
    out_ref[...] = jnp.concatenate(hidden, axis=0).T.astype(BF)


def hidden_of(first, second, own, other):
    count = 2 * first.shape[0] * first.shape[1]
    both = own.shape[0]
    return pl.pallas_call(
        up_kernel,
        grid=(1,),
        in_specs=[
            pl.BlockSpec(first.shape, lambda i: (0, 0, 0)),
            *whole(2),
            pl.BlockSpec((both, own.shape[1]), lambda i: (0, 0)),
        ],
        out_specs=whole(1)[0],
        out_shape=jax.ShapeDtypeStruct((count, both), BF),
        compiler_params=pltpu.CompilerParams(vmem_limit_bytes=24 << 20),
    )(first, second, own, other)


def down_kernel(place_ref, hidden_ref, shares_ref, out_ref):
    shares, cores, line = shares_ref.shape[:3]
    experts, _, slots, columns = out_ref.shape
    total = jnp.zeros((line * experts * slots, columns), F32)
    for at in range(line):
        k = place_ref[0] ^ at
        weights = [
            shares_ref[y, place_ref[1] ^ core, k] for core in range(cores) for y in range(shares)
        ]
        weights = jnp.concatenate(weights, axis=0)
        total += jnp.dot(hidden_ref[at], weights, preferred_element_type=F32)
    half = experts // 2
    total = total.astype(BF).reshape(2, line, half, slots, columns)
    for part in range(2):
        for p in range(line):
            out_ref[part * half : (part + 1) * half, p] = total[part, p]


def outputs_of(place, hidden, shares, experts, slots):
    return pl.pallas_call(
        down_kernel,
        in_specs=[pl.BlockSpec(memory_space=pltpu.SMEM)] + whole(2),
        out_specs=whole(1)[0],
        out_shape=jax.ShapeDtypeStruct((experts, hidden.shape[0], slots, shares.shape[-1]), BF),
        compiler_params=pltpu.CompilerParams(vmem_limit_bytes=16 << 20),
    )(place, hidden, shares)


def on_device(tokens, expert_ids, gate_scores, expert_weights):
    batches, row_count, width = tokens.shape
    experts = lax.axis_size("x") * lax.axis_size("zb")
    line = lax.axis_size("zi")
    capacity = 2
    slots = batches * capacity
    columns = width // line
    turned = expert_weights[0].T
    units = turned.shape[0] // 3
    place = lax.axis_index("zi")
    share = units // lax.axis_size("dp")
    down = lax.dynamic_slice_in_dim(turned, 2 * units + share * lax.axis_index("dp"), share, 0)
    down = down.reshape(share, line, columns)

    def for_place(at):
        return lax.dynamic_index_in_dim(down, at, 1, keepdims=False)

    pieces = [for_place(place)] + [exchange(for_place(place ^ k), "zi", k) for k in range(1, line)]
    packed, weighting = packed_of(expert_ids, gate_scores, tokens, experts, slots)
    mark = weighting[0, 0, 0, 0]
    up = jnp.where(mark == mark, turned[: 2 * units], jnp.zeros((), BF))
    other = swap(up)
    arrived = lax.all_to_all(packed, ROWS_OF, split_axis=0, concat_axis=0, tiled=True)
    half = experts // 2
    first = lax.all_gather(arrived[:half], "zi", axis=0, tiled=True)
    second = lax.all_gather(arrived[half:], "zi", axis=0, tiled=True)
    replicas, cores = lax.axis_size("dp"), lax.axis_size("c")
    shares = repeat_after(first, pieces, replicas * cores)
    shares = lax.all_to_all(shares, ("dp", "c"), split_axis=0, concat_axis=0, tiled=True)
    shares = shares.reshape((replicas, cores) + shares.shape[1:])
    hidden = hidden_of(first, second, up, other)
    gathered = lax.all_gather(hidden, "zi", axis=0)
    position = jnp.stack([place, lax.axis_index("c")]).astype(jnp.int32)
    done = outputs_of(position, gathered, shares, experts, slots)
    done = done.reshape(experts * line, slots, columns)
    returned = lax.all_to_all(done, HOME, split_axis=0, concat_axis=0, tiled=True)
    returned = returned.reshape(experts, line, batches, capacity, columns).astype(F32)
    mixed = jnp.einsum("mser,ezmsd->mrzd", weighting, returned, precision=lax.Precision.HIGHEST)
    return mixed.astype(BF).reshape(batches, row_count, width)


def solution(mesh):
    fine = Mesh(mesh.devices.reshape(4, 4, 4, 2, 4), ("x", "zb", "zi", "c", "dp"))
    ep = ("x", "zb", "zi", "c")
    by_row = P(None, ("dp",) + ep, None)
    return jax.shard_map(
        on_device,
        mesh=fine,
        in_specs=(by_row, by_row, by_row, P(ep, None, None)),
        out_specs=by_row,
        check_vma=False,
    )
```

```python
import jax
import jax.numpy as jnp
from jax import lax
from jax.experimental import pallas as pl
from jax.experimental.pallas import tpu as pltpu
from jax.sharding import Mesh, PartitionSpec as P

FF = 1536
BF = jnp.bfloat16
F32 = jnp.float32
ROWS_OF = ("x", "zb")
HOME = ("x", "zb", "zi")
ANYWHERE = pl.BlockSpec(memory_space=pl.ANY)
NT = (((1,), (1,)), ((), ()))


def exchange(array, axis, step):
    size = lax.axis_size(axis)
    return lax.ppermute(array, axis, [(i, i ^ step) for i in range(size)])


def swap(array):
    return lax.ppermute(array, "c", [(0, 1), (1, 0)])


def pack_kernel(ids_ref, gates_ref, tokens_ref, out_ref, weights_ref):
    batches, picks, rows = ids_ref.shape
    experts, slots, width = out_ref.shape
    capacity = slots // batches
    count = experts * slots
    expert = lax.broadcasted_iota(jnp.int32, (experts, rows), 0)
    row = lax.broadcasted_iota(jnp.int32, (rows, rows), 0)
    earlier = (row < lax.broadcasted_iota(jnp.int32, (rows, rows), 1)).astype(F32)
    owner = lax.broadcasted_iota(jnp.int32, (count, experts), 0) // slots
    spread = (owner == lax.broadcasted_iota(jnp.int32, (count, experts), 1)).astype(F32)
    slot = lax.broadcasted_iota(jnp.int32, (count, rows), 0) % slots
    total = jnp.zeros((count, width), F32)
    for m in range(batches):
        ids, gates = ids_ref[m], gates_ref[m]
        named = jnp.zeros((experts, rows), jnp.bool_)
        weight = jnp.zeros((experts, rows), F32)
        for k in range(picks):
            hit = ids[k : k + 1] == expert
            named = named | hit
            weight = jnp.where(hit, gates[k : k + 1], weight)
        named = named.astype(F32)
        before = jnp.dot(named, earlier, preferred_element_type=F32)
        for s in range(capacity):
            weights_ref[m, s] = jnp.where(before == s, weight, 0.0)
        named = jnp.dot(spread, named, preferred_element_type=F32)
        before = jnp.dot(spread, before, preferred_element_type=F32)
        here = (slot // capacity == m) & (before == (slot % capacity).astype(F32))
        pick = ((named > 0.5) & here).astype(BF)
        total += jnp.dot(pick, tokens_ref[m], preferred_element_type=F32)
    out_ref[...] = total.astype(BF).reshape(out_ref.shape)


def whole(count):
    return [pl.BlockSpec(memory_space=pltpu.VMEM)] * count


def packed_of(expert_ids, gate_scores, tokens, experts, slots):
    batches, rows, width = tokens.shape
    return pl.pallas_call(
        pack_kernel,
        in_specs=whole(3),
        out_specs=whole(2),
        out_shape=[
            jax.ShapeDtypeStruct((experts, slots, width), BF),
            jax.ShapeDtypeStruct((batches, slots // batches, experts, rows), F32),
        ],
        compiler_params=pltpu.CompilerParams(vmem_limit_bytes=16 << 20),
    )(expert_ids.transpose(0, 2, 1), gate_scores.transpose(0, 2, 1), tokens)


def repeat_kernel(_, *refs):
    arrays, out_ref, done = refs[:-2], refs[-2], refs[-1]
    copies = [
        pltpu.make_async_copy(ref, out_ref.at[copy, k], done.at[copy, k])
        for copy in range(out_ref.shape[0])
        for k, ref in enumerate(arrays)
    ]
    for copy in copies:
        copy.start()
    for copy in copies:
        copy.wait()


def repeat_after(earlier, arrays, times):
    return pl.pallas_call(
        repeat_kernel,
        in_specs=[ANYWHERE] + whole(len(arrays)),
        out_specs=pl.BlockSpec(memory_space=pltpu.HBM),
        out_shape=jax.ShapeDtypeStruct((times, len(arrays)) + arrays[0].shape, BF),
        scratch_shapes=[pltpu.SemaphoreType.DMA((times, len(arrays)))],
        compiler_params=pltpu.CompilerParams(vmem_limit_bytes=53 << 20),
    )(earlier, *arrays)


def copy_kernel(_, array_ref, out_ref):
    out_ref[...] = array_ref[...]


def copy_after(earlier, array):
    return pl.pallas_call(
        copy_kernel,
        in_specs=[ANYWHERE] + whole(1),
        out_specs=whole(1)[0],
        out_shape=jax.ShapeDtypeStruct(array.shape, array.dtype),
        compiler_params=pltpu.CompilerParams(vmem_limit_bytes=16 << 20),
    )(earlier, array)


def up_kernel(first_ref, second_ref, own_ref, other_ref, out_ref):
    units = own_ref.shape[0] // 3
    width = own_ref.shape[1]
    rows = [ref[...].reshape(-1, width) for ref in (first_ref, second_ref)]
    rows = jnp.concatenate(rows, axis=0)
    hidden = []
    for ref in (own_ref, other_ref):
        both = lax.dot_general(ref[: 2 * units], rows, NT, preferred_element_type=F32)
        gate = both[:units]
        hidden.append(gate / (1.0 + jnp.exp(-gate)) * both[units:])
    out_ref[...] = jnp.concatenate(hidden, axis=0).T.astype(BF)


def hidden_of(first, second, own, other):
    count = 2 * first.shape[0] * first.shape[1]
    both = own.shape[0] // 3 * 2
    return pl.pallas_call(
        up_kernel,
        grid=(1,),
        in_specs=whole(3) + [pl.BlockSpec((both, own.shape[1]), lambda i: (0, 0))],
        out_specs=whole(1)[0],
        out_shape=jax.ShapeDtypeStruct((count, both), BF),
        compiler_params=pltpu.CompilerParams(vmem_limit_bytes=24 << 20),
    )(first, second, own, other)


def down_kernel(place_ref, hidden_ref, shares_ref, out_ref):
    shares, cores, line = shares_ref.shape[:3]
    experts, _, slots, columns = out_ref.shape
    total = jnp.zeros((line * experts * slots, columns), F32)
    for at in range(line):
        k = place_ref[0] ^ at
        weights = [
            shares_ref[y, place_ref[1] ^ core, k] for core in range(cores) for y in range(shares)
        ]
        weights = jnp.concatenate(weights, axis=0)
        total += jnp.dot(hidden_ref[at], weights, preferred_element_type=F32)
    half = experts // 2
    total = total.astype(BF).reshape(2, line, half, slots, columns)
    for part in range(2):
        for p in range(line):
            out_ref[part * half : (part + 1) * half, p] = total[part, p]


def outputs_of(place, hidden, shares, experts, slots):
    return pl.pallas_call(
        down_kernel,
        in_specs=[pl.BlockSpec(memory_space=pltpu.SMEM)] + whole(2),
        out_specs=whole(1)[0],
        out_shape=jax.ShapeDtypeStruct((experts, hidden.shape[0], slots, shares.shape[-1]), BF),
        compiler_params=pltpu.CompilerParams(vmem_limit_bytes=16 << 20),
    )(place, hidden, shares)


def on_device(tokens, expert_ids, gate_scores, expert_weights):
    batches, row_count, width = tokens.shape
    experts = lax.axis_size("x") * lax.axis_size("zb")
    line = lax.axis_size("zi")
    capacity = 2
    slots = batches * capacity
    columns = width // line
    turned = expert_weights[0].T
    units = turned.shape[0] // 3
    place = lax.axis_index("zi")
    share = units // lax.axis_size("dp")
    down = lax.dynamic_slice_in_dim(turned, 2 * units + share * lax.axis_index("dp"), share, 0)
    down = down.reshape(share, line, columns)

    def for_place(at):
        return lax.dynamic_index_in_dim(down, at, 1, keepdims=False)

    pieces = [for_place(place)] + [exchange(for_place(place ^ k), "zi", k) for k in range(1, line)]
    packed, weighting = packed_of(expert_ids, gate_scores, tokens, experts, slots)
    mark = weighting[0, 0, 0, 0]
    up = jnp.where(mark == mark, turned[: 2 * units], jnp.zeros((), BF))
    other = swap(up)
    arrived = lax.all_to_all(packed, ROWS_OF, split_axis=0, concat_axis=0, tiled=True)
    replicas, cores = lax.axis_size("dp"), lax.axis_size("c")
    shares = repeat_after(arrived, pieces, replicas * cores)
    shares = lax.all_to_all(shares, ("dp", "c"), split_axis=0, concat_axis=0, tiled=True)
    shares = shares.reshape((replicas, cores) + shares.shape[1:])
    half = experts // 2
    first = lax.all_gather(arrived[:half], "zi", axis=0, tiled=True)
    later = copy_after(first, arrived[half:])
    second = lax.all_gather(later, "zi", axis=0, tiled=True)
    hidden = hidden_of(first, second, turned, other)
    gathered = lax.all_gather(hidden, "zi", axis=0)
    position = jnp.stack([place, lax.axis_index("c")]).astype(jnp.int32)
    done = outputs_of(position, gathered, shares, experts, slots)
    done = done.reshape(experts * line, slots, columns)
    returned = lax.all_to_all(done, HOME, split_axis=0, concat_axis=0, tiled=True)
    returned = returned.reshape(experts, line, batches, capacity, columns).astype(F32)
    mixed = jnp.einsum("mser,ezmsd->mrzd", weighting, returned, precision=lax.Precision.HIGHEST)
    return mixed.astype(BF).reshape(batches, row_count, width)


def solution(mesh):
    fine = Mesh(mesh.devices.reshape(4, 4, 4, 2, 4), ("x", "zb", "zi", "c", "dp"))
    ep = ("x", "zb", "zi", "c")
    by_row = P(None, ("dp",) + ep, None)
    return jax.shard_map(
        on_device,
        mesh=fine,
        in_specs=(by_row, by_row, by_row, P(ep, None, None)),
        out_specs=by_row,
        check_vma=False,
    )
```

```python
import functools

import jax
import jax.numpy as jnp
from jax import lax
from jax.experimental import pallas as pl
from jax.experimental.pallas import tpu as pltpu
from jax.sharding import Mesh, PartitionSpec as P

FF = 1536
BF = jnp.bfloat16
F32 = jnp.float32
ROWS_OF = ("zb", "x")
HOME = ("zb", "x", "zi")
ANYWHERE = pl.BlockSpec(memory_space=pl.ANY)
NT = (((1,), (1,)), ((), ()))


def exchange(array, axis, step):
    size = lax.axis_size(axis)
    return lax.ppermute(array, axis, [(i, i ^ step) for i in range(size)])


def swap(array):
    return lax.ppermute(array, "c", [(0, 1), (1, 0)])


def pack_kernel(sides, ids_ref, gates_ref, tokens_ref, out_ref, weights_ref):
    batches, picks, rows = ids_ref.shape
    experts, slots, width = out_ref.shape
    capacity = slots // batches
    count = experts * slots
    at = lax.broadcasted_iota(jnp.int32, (experts, rows), 0)
    expert = at % sides[0] * sides[1] + at // sides[0]
    row = lax.broadcasted_iota(jnp.int32, (rows, rows), 0)
    earlier = (row < lax.broadcasted_iota(jnp.int32, (rows, rows), 1)).astype(F32)
    owner = lax.broadcasted_iota(jnp.int32, (count, experts), 0) // slots
    spread = (owner == lax.broadcasted_iota(jnp.int32, (count, experts), 1)).astype(F32)
    slot = lax.broadcasted_iota(jnp.int32, (count, rows), 0) % slots
    total = jnp.zeros((count, width), F32)
    for m in range(batches):
        ids, gates = ids_ref[m], gates_ref[m]
        named = jnp.zeros((experts, rows), jnp.bool_)
        weight = jnp.zeros((experts, rows), F32)
        for k in range(picks):
            hit = ids[k : k + 1] == expert
            named = named | hit
            weight = jnp.where(hit, gates[k : k + 1], weight)
        named = named.astype(F32)
        before = jnp.dot(named, earlier, preferred_element_type=F32)
        for s in range(capacity):
            weights_ref[m, s] = jnp.where(before == s, weight, 0.0)
        named = jnp.dot(spread, named, preferred_element_type=F32)
        before = jnp.dot(spread, before, preferred_element_type=F32)
        here = (slot // capacity == m) & (before == (slot % capacity).astype(F32))
        pick = ((named > 0.5) & here).astype(BF)
        total += jnp.dot(pick, tokens_ref[m], preferred_element_type=F32)
    out_ref[...] = total.astype(BF).reshape(out_ref.shape)


def whole(count):
    return [pl.BlockSpec(memory_space=pltpu.VMEM)] * count


def packed_of(expert_ids, gate_scores, tokens, experts, slots):
    batches, rows, width = tokens.shape
    sides = (lax.axis_size("x"), lax.axis_size("zb"))
    return pl.pallas_call(
        functools.partial(pack_kernel, sides),
        in_specs=whole(3),
        out_specs=whole(2),
        out_shape=[
            jax.ShapeDtypeStruct((experts, slots, width), BF),
            jax.ShapeDtypeStruct((batches, slots // batches, experts, rows), F32),
        ],
        compiler_params=pltpu.CompilerParams(vmem_limit_bytes=16 << 20),
    )(expert_ids.transpose(0, 2, 1), gate_scores.transpose(0, 2, 1), tokens)


def repeat_kernel(_, *refs):
    arrays, out_ref, done = refs[:-2], refs[-2], refs[-1]
    copies = [
        pltpu.make_async_copy(ref, out_ref.at[copy, k], done.at[copy, k])
        for copy in range(out_ref.shape[0])
        for k, ref in enumerate(arrays)
    ]
    for copy in copies:
        copy.start()
    for copy in copies:
        copy.wait()


def repeat_after(earlier, arrays, times):
    return pl.pallas_call(
        repeat_kernel,
        in_specs=[ANYWHERE] + whole(len(arrays)),
        out_specs=pl.BlockSpec(memory_space=pltpu.HBM),
        out_shape=jax.ShapeDtypeStruct((times, len(arrays)) + arrays[0].shape, BF),
        scratch_shapes=[pltpu.SemaphoreType.DMA((times, len(arrays)))],
        compiler_params=pltpu.CompilerParams(vmem_limit_bytes=53 << 20),
    )(earlier, *arrays)


def copy_kernel(_, array_ref, out_ref):
    out_ref[...] = array_ref[...]


def copy_after(earlier, array):
    return pl.pallas_call(
        copy_kernel,
        in_specs=[ANYWHERE] + whole(1),
        out_specs=whole(1)[0],
        out_shape=jax.ShapeDtypeStruct(array.shape, array.dtype),
        compiler_params=pltpu.CompilerParams(vmem_limit_bytes=16 << 20),
    )(earlier, array)


def up_kernel(first_ref, second_ref, own_ref, other_ref, out_ref):
    units = own_ref.shape[0] // 3
    width = own_ref.shape[1]
    rows = [ref[...].reshape(-1, width) for ref in (first_ref, second_ref)]
    rows = jnp.concatenate(rows, axis=0)
    hidden = []
    for ref in (own_ref, other_ref):
        both = lax.dot_general(ref[: 2 * units], rows, NT, preferred_element_type=F32)
        gate = both[:units]
        hidden.append(gate / (1.0 + jnp.exp(-gate)) * both[units:])
    out_ref[...] = jnp.concatenate(hidden, axis=0).T.astype(BF)


def hidden_of(first, second, own, other):
    count = 2 * first.shape[0] * first.shape[1]
    both = own.shape[0] // 3 * 2
    return pl.pallas_call(
        up_kernel,
        grid=(1,),
        in_specs=whole(3) + [pl.BlockSpec((both, own.shape[1]), lambda i: (0, 0))],
        out_specs=whole(1)[0],
        out_shape=jax.ShapeDtypeStruct((count, both), BF),
        compiler_params=pltpu.CompilerParams(vmem_limit_bytes=24 << 20),
    )(first, second, own, other)


def down_kernel(place_ref, hidden_ref, shares_ref, out_ref):
    shares, cores, line = shares_ref.shape[:3]
    experts, _, slots, columns = out_ref.shape
    total = jnp.zeros((line * experts * slots, columns), F32)
    for at in range(line):
        k = place_ref[0] ^ at
        weights = [
            shares_ref[y, place_ref[1] ^ core, k] for core in range(cores) for y in range(shares)
        ]
        weights = jnp.concatenate(weights, axis=0)
        total += jnp.dot(hidden_ref[at], weights, preferred_element_type=F32)
    half = experts // 2
    total = total.astype(BF).reshape(2, line, half, slots, columns)
    for part in range(2):
        for p in range(line):
            out_ref[part * half : (part + 1) * half, p] = total[part, p]


def outputs_of(place, hidden, shares, experts, slots):
    return pl.pallas_call(
        down_kernel,
        in_specs=[pl.BlockSpec(memory_space=pltpu.SMEM)] + whole(2),
        out_specs=whole(1)[0],
        out_shape=jax.ShapeDtypeStruct((experts, hidden.shape[0], slots, shares.shape[-1]), BF),
        compiler_params=pltpu.CompilerParams(vmem_limit_bytes=16 << 20),
    )(place, hidden, shares)


def on_device(tokens, expert_ids, gate_scores, expert_weights):
    batches, row_count, width = tokens.shape
    experts = lax.axis_size("x") * lax.axis_size("zb")
    line = lax.axis_size("zi")
    capacity = 2
    slots = batches * capacity
    columns = width // line
    turned = expert_weights[0].T
    units = turned.shape[0] // 3
    place = lax.axis_index("zi")
    share = units // lax.axis_size("dp")
    down = lax.dynamic_slice_in_dim(turned, 2 * units + share * lax.axis_index("dp"), share, 0)
    down = down.reshape(share, line, columns)

    def for_place(at):
        return lax.dynamic_index_in_dim(down, at, 1, keepdims=False)

    pieces = [for_place(place)] + [exchange(for_place(place ^ k), "zi", k) for k in range(1, line)]
    packed, weighting = packed_of(expert_ids, gate_scores, tokens, experts, slots)
    mark = weighting[0, 0, 0, 0]
    up = jnp.where(mark == mark, turned[: 2 * units], jnp.zeros((), BF))
    other = swap(up)
    arrived = lax.all_to_all(packed, ROWS_OF, split_axis=0, concat_axis=0, tiled=True)
    replicas, cores = lax.axis_size("dp"), lax.axis_size("c")
    shares = repeat_after(arrived, pieces, replicas * cores)
    shares = lax.all_to_all(shares, ("dp", "c"), split_axis=0, concat_axis=0, tiled=True)
    shares = shares.reshape((replicas, cores) + shares.shape[1:])
    half = experts // 2
    first = lax.all_gather(arrived[:half], "zi", axis=0, tiled=True)
    later = copy_after(first, arrived[half:])
    second = lax.all_gather(later, "zi", axis=0, tiled=True)
    hidden = hidden_of(first, second, turned, other)
    gathered = lax.all_gather(hidden, "zi", axis=0)
    position = jnp.stack([place, lax.axis_index("c")]).astype(jnp.int32)
    done = outputs_of(position, gathered, shares, experts, slots)
    done = done.reshape(experts * line, slots, columns)
    returned = lax.all_to_all(done, HOME, split_axis=0, concat_axis=0, tiled=True)
    returned = returned.reshape(experts, line, batches, capacity, columns).astype(F32)
    mixed = jnp.einsum("mser,ezmsd->mrzd", weighting, returned, precision=lax.Precision.HIGHEST)
    return mixed.astype(BF).reshape(batches, row_count, width)


def solution(mesh):
    fine = Mesh(mesh.devices.reshape(4, 4, 4, 2, 4), ("x", "zb", "zi", "c", "dp"))
    ep = ("x", "zb", "zi", "c")
    by_row = P(None, ("dp",) + ep, None)
    return jax.shard_map(
        on_device,
        mesh=fine,
        in_specs=(by_row, by_row, by_row, P(ep, None, None)),
        out_specs=by_row,
        check_vma=False,
    )
```

```python
import functools

import jax
import jax.numpy as jnp
from jax import lax
from jax.experimental import pallas as pl
from jax.experimental.pallas import tpu as pltpu
from jax.sharding import Mesh, PartitionSpec as P

FF = 1536
BF = jnp.bfloat16
F32 = jnp.float32
ROWS_OF = ("zb", "x")
HOME = ("x", "zb", "zi")
ANYWHERE = pl.BlockSpec(memory_space=pl.ANY)
NT = (((1,), (1,)), ((), ()))


def exchange(array, axis, step):
    size = lax.axis_size(axis)
    return lax.ppermute(array, axis, [(i, i ^ step) for i in range(size)])


def swap(array):
    return lax.ppermute(array, "c", [(0, 1), (1, 0)])


def named_in(ids, expert):
    rows = ids.shape[1]
    row = lax.broadcasted_iota(jnp.int32, (rows, rows), 0)
    earlier = (row < lax.broadcasted_iota(jnp.int32, (rows, rows), 1)).astype(F32)
    hits = [ids[k : k + 1] == expert for k in range(ids.shape[0])]
    named = jnp.zeros(expert.shape, jnp.bool_)
    for hit in hits:
        named = named | hit
    named = named.astype(F32)
    return hits, named, jnp.dot(named, earlier, preferred_element_type=F32)


def pack_kernel(sides, ids_ref, gates_ref, tokens_ref, out_ref, weights_ref):
    batches, _, rows = ids_ref.shape
    experts, slots, width = out_ref.shape
    capacity = slots // batches
    count = experts * slots
    expert = lax.broadcasted_iota(jnp.int32, (experts, rows), 0)
    sent = expert % sides[0] * sides[1] + expert // sides[0]
    owner = lax.broadcasted_iota(jnp.int32, (count, experts), 0) // slots
    spread = (owner == lax.broadcasted_iota(jnp.int32, (count, experts), 1)).astype(F32)
    slot = lax.broadcasted_iota(jnp.int32, (count, rows), 0) % slots
    total = jnp.zeros((count, width), F32)
    for m in range(batches):
        hits, _, before = named_in(ids_ref[m], expert)
        weight = jnp.zeros((experts, rows), F32)
        for k, hit in enumerate(hits):
            weight = jnp.where(hit, gates_ref[m, k : k + 1], weight)
        for s in range(capacity):
            weights_ref[m, s] = jnp.where(before == s, weight, 0.0)
        _, named, before = named_in(ids_ref[m], sent)
        named = jnp.dot(spread, named, preferred_element_type=F32)
        before = jnp.dot(spread, before, preferred_element_type=F32)
        here = (slot // capacity == m) & (before == (slot % capacity).astype(F32))
        pick = ((named > 0.5) & here).astype(BF)
        total += jnp.dot(pick, tokens_ref[m], preferred_element_type=F32)
    out_ref[...] = total.astype(BF).reshape(out_ref.shape)


def whole(count):
    return [pl.BlockSpec(memory_space=pltpu.VMEM)] * count


def packed_of(expert_ids, gate_scores, tokens, experts, slots):
    batches, rows, width = tokens.shape
    sides = (lax.axis_size("x"), lax.axis_size("zb"))
    return pl.pallas_call(
        functools.partial(pack_kernel, sides),
        in_specs=whole(3),
        out_specs=whole(2),
        out_shape=[
            jax.ShapeDtypeStruct((experts, slots, width), BF),
            jax.ShapeDtypeStruct((batches, slots // batches, experts, rows), F32),
        ],
        compiler_params=pltpu.CompilerParams(vmem_limit_bytes=16 << 20),
    )(expert_ids.transpose(0, 2, 1), gate_scores.transpose(0, 2, 1), tokens)


def repeat_kernel(_, *refs):
    arrays, out_ref, done = refs[:-2], refs[-2], refs[-1]
    copies = [
        pltpu.make_async_copy(ref, out_ref.at[copy, k], done.at[copy, k])
        for copy in range(out_ref.shape[0])
        for k, ref in enumerate(arrays)
    ]
    for copy in copies:
        copy.start()
    for copy in copies:
        copy.wait()


def repeat_after(earlier, arrays, times):
    return pl.pallas_call(
        repeat_kernel,
        in_specs=[ANYWHERE] + whole(len(arrays)),
        out_specs=pl.BlockSpec(memory_space=pltpu.HBM),
        out_shape=jax.ShapeDtypeStruct((times, len(arrays)) + arrays[0].shape, BF),
        scratch_shapes=[pltpu.SemaphoreType.DMA((times, len(arrays)))],
        compiler_params=pltpu.CompilerParams(vmem_limit_bytes=53 << 20),
    )(earlier, *arrays)


def copy_kernel(_, array_ref, out_ref):
    out_ref[...] = array_ref[...]


def copy_after(earlier, array):
    return pl.pallas_call(
        copy_kernel,
        in_specs=[ANYWHERE] + whole(1),
        out_specs=whole(1)[0],
        out_shape=jax.ShapeDtypeStruct(array.shape, array.dtype),
        compiler_params=pltpu.CompilerParams(vmem_limit_bytes=16 << 20),
    )(earlier, array)


def up_kernel(first_ref, second_ref, own_ref, other_ref, out_ref):
    units = own_ref.shape[0] // 3
    width = own_ref.shape[1]
    rows = [ref[...].reshape(-1, width) for ref in (first_ref, second_ref)]
    rows = jnp.concatenate(rows, axis=0)
    hidden = []
    for ref in (own_ref, other_ref):
        both = lax.dot_general(ref[: 2 * units], rows, NT, preferred_element_type=F32)
        gate = both[:units]
        hidden.append(gate / (1.0 + jnp.exp(-gate)) * both[units:])
    out_ref[...] = jnp.concatenate(hidden, axis=0).T.astype(BF)


def hidden_of(first, second, own, other):
    count = 2 * first.shape[0] * first.shape[1]
    both = own.shape[0] // 3 * 2
    return pl.pallas_call(
        up_kernel,
        grid=(1,),
        in_specs=whole(3) + [pl.BlockSpec((both, own.shape[1]), lambda i: (0, 0))],
        out_specs=whole(1)[0],
        out_shape=jax.ShapeDtypeStruct((count, both), BF),
        compiler_params=pltpu.CompilerParams(vmem_limit_bytes=24 << 20),
    )(first, second, own, other)


def down_kernel(place_ref, hidden_ref, shares_ref, out_ref):
    shares, cores, line = shares_ref.shape[:3]
    across, blocks, _, slots, columns = out_ref.shape
    half = across * blocks // 2
    total = jnp.zeros((2 * line * half * slots, columns), F32)
    for at in range(line):
        k = place_ref[0] ^ at
        weights = [
            shares_ref[y, place_ref[1] ^ core, k] for core in range(cores) for y in range(shares)
        ]
        weights = jnp.concatenate(weights, axis=0)
        total += jnp.dot(hidden_ref[at], weights, preferred_element_type=F32)
    total = total.astype(BF).reshape(2, line, blocks // 2, across, slots, columns)
    for block in range(blocks):
        for p in range(line):
            out_ref[:, block, p] = total[block // (blocks // 2), p, block % (blocks // 2)]


def outputs_of(place, hidden, shares, slots):
    sides = (lax.axis_size("x"), lax.axis_size("zb"))
    line, columns = hidden.shape[0], shares.shape[-1]
    return pl.pallas_call(
        down_kernel,
        in_specs=[pl.BlockSpec(memory_space=pltpu.SMEM)] + whole(2),
        out_specs=whole(1)[0],
        out_shape=jax.ShapeDtypeStruct(sides + (line, slots, columns), BF),
        compiler_params=pltpu.CompilerParams(vmem_limit_bytes=16 << 20),
    )(place, hidden, shares)


def on_device(tokens, expert_ids, gate_scores, expert_weights):
    batches, row_count, width = tokens.shape
    experts = lax.axis_size("x") * lax.axis_size("zb")
    line = lax.axis_size("zi")
    capacity = 2
    slots = batches * capacity
    columns = width // line
    turned = expert_weights[0].T
    units = turned.shape[0] // 3
    place = lax.axis_index("zi")
    share = units // lax.axis_size("dp")
    down = lax.dynamic_slice_in_dim(turned, 2 * units + share * lax.axis_index("dp"), share, 0)
    down = down.reshape(share, line, columns)

    def for_place(at):
        return lax.dynamic_index_in_dim(down, at, 1, keepdims=False)

    pieces = [for_place(place)] + [exchange(for_place(place ^ k), "zi", k) for k in range(1, line)]
    packed, weighting = packed_of(expert_ids, gate_scores, tokens, experts, slots)
    mark = weighting[0, 0, 0, 0]
    up = jnp.where(mark == mark, turned[: 2 * units], jnp.zeros((), BF))
    other = swap(up)
    arrived = lax.all_to_all(packed, ROWS_OF, split_axis=0, concat_axis=0, tiled=True)
    replicas, cores = lax.axis_size("dp"), lax.axis_size("c")
    shares = repeat_after(arrived, pieces, replicas * cores)
    shares = lax.all_to_all(shares, ("dp", "c"), split_axis=0, concat_axis=0, tiled=True)
    shares = shares.reshape((replicas, cores) + shares.shape[1:])
    half = experts // 2
    first = lax.all_gather(arrived[:half], "zi", axis=0, tiled=True)
    later = copy_after(first, arrived[half:])
    second = lax.all_gather(later, "zi", axis=0, tiled=True)
    hidden = hidden_of(first, second, turned, other)
    gathered = lax.all_gather(hidden, "zi", axis=0)
    position = jnp.stack([place, lax.axis_index("c")]).astype(jnp.int32)
    done = outputs_of(position, gathered, shares, slots)
    done = done.reshape(experts * line, slots, columns)
    returned = lax.all_to_all(done, HOME, split_axis=0, concat_axis=0, tiled=True)
    returned = returned.reshape(experts, line, batches, capacity, columns).astype(F32)
    mixed = jnp.einsum("mser,ezmsd->mrzd", weighting, returned, precision=lax.Precision.HIGHEST)
    return mixed.astype(BF).reshape(batches, row_count, width)


def solution(mesh):
    fine = Mesh(mesh.devices.reshape(4, 4, 4, 2, 4), ("x", "zb", "zi", "c", "dp"))
    ep = ("x", "zb", "zi", "c")
    by_row = P(None, ("dp",) + ep, None)
    return jax.shard_map(
        on_device,
        mesh=fine,
        in_specs=(by_row, by_row, by_row, P(ep, None, None)),
        out_specs=by_row,
        check_vma=False,
    )
```

```python
import jax
import jax.numpy as jnp
from jax import lax
from jax.experimental import pallas as pl
from jax.experimental.pallas import tpu as pltpu
from jax.sharding import Mesh, PartitionSpec as P

FF = 1536
BF = jnp.bfloat16
F32 = jnp.float32
ROWS_OF = ("x", "zb")
HOME = ("x", "zb", "zi")
ANYWHERE = pl.BlockSpec(memory_space=pl.ANY)
NT = (((1,), (1,)), ((), ()))


def exchange(array, axis, step):
    size = lax.axis_size(axis)
    return lax.ppermute(array, axis, [(i, i ^ step) for i in range(size)])


def swap(array):
    return lax.ppermute(array, "c", [(0, 1), (1, 0)])


def named_in(ids, experts):
    rows = ids.shape[1]
    expert = lax.broadcasted_iota(jnp.int32, (experts, rows), 0)
    row = lax.broadcasted_iota(jnp.int32, (rows, rows), 0)
    earlier = (row < lax.broadcasted_iota(jnp.int32, (rows, rows), 1)).astype(F32)
    hits = [ids[k : k + 1] == expert for k in range(ids.shape[0])]
    named = jnp.zeros((experts, rows), jnp.bool_)
    for hit in hits:
        named = named | hit
    named = named.astype(F32)
    return hits, named, jnp.dot(named, earlier, preferred_element_type=F32)


def pack_kernel(ids_ref, tokens_ref, out_ref):
    batches, _, rows = ids_ref.shape
    experts, slots, width = out_ref.shape
    capacity = slots // batches
    count = experts * slots
    owner = lax.broadcasted_iota(jnp.int32, (count, experts), 0) // slots
    spread = (owner == lax.broadcasted_iota(jnp.int32, (count, experts), 1)).astype(F32)
    slot = lax.broadcasted_iota(jnp.int32, (count, rows), 0) % slots
    total = jnp.zeros((count, width), F32)
    for m in range(batches):
        _, named, before = named_in(ids_ref[m], experts)
        named = jnp.dot(spread, named, preferred_element_type=F32)
        before = jnp.dot(spread, before, preferred_element_type=F32)
        here = (slot // capacity == m) & (before == (slot % capacity).astype(F32))
        pick = ((named > 0.5) & here).astype(BF)
        total += jnp.dot(pick, tokens_ref[m], preferred_element_type=F32)
    out_ref[...] = total.astype(BF).reshape(out_ref.shape)


def whole(count):
    return [pl.BlockSpec(memory_space=pltpu.VMEM)] * count


def packed_of(expert_ids, tokens, experts, slots):
    return pl.pallas_call(
        pack_kernel,
        in_specs=whole(2),
        out_specs=whole(1)[0],
        out_shape=jax.ShapeDtypeStruct((experts, slots, tokens.shape[2]), BF),
        compiler_params=pltpu.CompilerParams(vmem_limit_bytes=16 << 20),
    )(expert_ids.transpose(0, 2, 1), tokens)


def repeat_kernel(_, ids_ref, gates_ref, *refs):
    arrays, out_ref, weights_ref, done = refs[:-3], refs[-3], refs[-2], refs[-1]
    copies = [
        pltpu.make_async_copy(ref, out_ref.at[copy, k], done.at[copy, k])
        for copy in range(out_ref.shape[0])
        for k, ref in enumerate(arrays)
    ]
    for copy in copies:
        copy.start()
    batches, capacity, experts, rows = weights_ref.shape
    for m in range(batches):
        hits, _, before = named_in(ids_ref[m], experts)
        weight = jnp.zeros((experts, rows), F32)
        for k, hit in enumerate(hits):
            weight = jnp.where(hit, gates_ref[m, k : k + 1], weight)
        for s in range(capacity):
            weights_ref[m, s] = jnp.where(before == s, weight, 0.0)
    for copy in copies:
        copy.wait()


def repeat_after(earlier, arrays, times, expert_ids, gate_scores, experts, capacity):
    batches, rows, _ = expert_ids.shape
    return pl.pallas_call(
        repeat_kernel,
        in_specs=[ANYWHERE] + whole(2 + len(arrays)),
        out_specs=[pl.BlockSpec(memory_space=pltpu.HBM)] + whole(1),
        out_shape=[
            jax.ShapeDtypeStruct((times, len(arrays)) + arrays[0].shape, BF),
            jax.ShapeDtypeStruct((batches, capacity, experts, rows), F32),
        ],
        scratch_shapes=[pltpu.SemaphoreType.DMA((times, len(arrays)))],
        compiler_params=pltpu.CompilerParams(vmem_limit_bytes=53 << 20),
    )(earlier, expert_ids.transpose(0, 2, 1), gate_scores.transpose(0, 2, 1), *arrays)


def copy_kernel(_, array_ref, out_ref):
    out_ref[...] = array_ref[...]


def copy_after(earlier, array):
    return pl.pallas_call(
        copy_kernel,
        in_specs=[ANYWHERE] + whole(1),
        out_specs=whole(1)[0],
        out_shape=jax.ShapeDtypeStruct(array.shape, array.dtype),
        compiler_params=pltpu.CompilerParams(vmem_limit_bytes=16 << 20),
    )(earlier, array)


def up_kernel(first_ref, second_ref, own_ref, other_ref, out_ref):
    units = own_ref.shape[0] // 3
    width = own_ref.shape[1]
    rows = [ref[...].reshape(-1, width) for ref in (first_ref, second_ref)]
    rows = jnp.concatenate(rows, axis=0)
    hidden = []
    for ref in (own_ref, other_ref):
        both = lax.dot_general(ref[: 2 * units], rows, NT, preferred_element_type=F32)
        gate = both[:units]
        hidden.append(gate / (1.0 + jnp.exp(-gate)) * both[units:])
    out_ref[...] = jnp.concatenate(hidden, axis=0).T.astype(BF)


def hidden_of(first, second, own, other):
    count = 2 * first.shape[0] * first.shape[1]
    both = own.shape[0] // 3 * 2
    return pl.pallas_call(
        up_kernel,
        grid=(1,),
        in_specs=whole(3) + [pl.BlockSpec((both, own.shape[1]), lambda i: (0, 0))],
        out_specs=whole(1)[0],
        out_shape=jax.ShapeDtypeStruct((count, both), BF),
        compiler_params=pltpu.CompilerParams(vmem_limit_bytes=24 << 20),
    )(first, second, own, other)


def down_kernel(place_ref, hidden_ref, shares_ref, out_ref):
    shares, cores, line = shares_ref.shape[:3]
    experts, _, slots, columns = out_ref.shape
    total = jnp.zeros((line * experts * slots, columns), F32)
    for at in range(line):
        k = place_ref[0] ^ at
        weights = [
            shares_ref[y, place_ref[1] ^ core, k] for core in range(cores) for y in range(shares)
        ]
        weights = jnp.concatenate(weights, axis=0)
        total += jnp.dot(hidden_ref[at], weights, preferred_element_type=F32)
    half = experts // 2
    total = total.astype(BF).reshape(2, line, half, slots, columns)
    for part in range(2):
        for p in range(line):
            out_ref[part * half : (part + 1) * half, p] = total[part, p]


def outputs_of(place, hidden, shares, experts, slots):
    return pl.pallas_call(
        down_kernel,
        in_specs=[pl.BlockSpec(memory_space=pltpu.SMEM)] + whole(2),
        out_specs=whole(1)[0],
        out_shape=jax.ShapeDtypeStruct((experts, hidden.shape[0], slots, shares.shape[-1]), BF),
        compiler_params=pltpu.CompilerParams(vmem_limit_bytes=16 << 20),
    )(place, hidden, shares)


def on_device(tokens, expert_ids, gate_scores, expert_weights):
    batches, row_count, width = tokens.shape
    experts = lax.axis_size("x") * lax.axis_size("zb")
    line = lax.axis_size("zi")
    capacity = 2
    slots = batches * capacity
    columns = width // line
    turned = expert_weights[0].T
    units = turned.shape[0] // 3
    place = lax.axis_index("zi")
    share = units // lax.axis_size("dp")
    down = lax.dynamic_slice_in_dim(turned, 2 * units + share * lax.axis_index("dp"), share, 0)
    down = down.reshape(share, line, columns)

    def for_place(at):
        return lax.dynamic_index_in_dim(down, at, 1, keepdims=False)

    pieces = [for_place(place)] + [exchange(for_place(place ^ k), "zi", k) for k in range(1, line)]
    packed = packed_of(expert_ids, tokens, experts, slots)
    mark = packed[0, 0, 0]
    up = jnp.where(mark == mark, turned[: 2 * units], jnp.zeros((), BF))
    other = swap(up)
    arrived = lax.all_to_all(packed, ROWS_OF, split_axis=0, concat_axis=0, tiled=True)
    replicas, cores = lax.axis_size("dp"), lax.axis_size("c")
    shares, weighting = repeat_after(
        arrived, pieces, replicas * cores, expert_ids, gate_scores, experts, capacity
    )
    shares = lax.all_to_all(shares, ("dp", "c"), split_axis=0, concat_axis=0, tiled=True)
    shares = shares.reshape((replicas, cores) + shares.shape[1:])
    half = experts // 2
    first = lax.all_gather(arrived[:half], "zi", axis=0, tiled=True)
    later = copy_after(first, arrived[half:])
    second = lax.all_gather(later, "zi", axis=0, tiled=True)
    hidden = hidden_of(first, second, turned, other)
    gathered = lax.all_gather(hidden, "zi", axis=0)
    position = jnp.stack([place, lax.axis_index("c")]).astype(jnp.int32)
    done = outputs_of(position, gathered, shares, experts, slots)
    done = done.reshape(experts * line, slots, columns)
    returned = lax.all_to_all(done, HOME, split_axis=0, concat_axis=0, tiled=True)
    returned = returned.reshape(experts, line, batches, capacity, columns).astype(F32)
    mixed = jnp.einsum("mser,ezmsd->mrzd", weighting, returned, precision=lax.Precision.HIGHEST)
    return mixed.astype(BF).reshape(batches, row_count, width)


def solution(mesh):
    fine = Mesh(mesh.devices.reshape(4, 4, 4, 2, 4), ("x", "zb", "zi", "c", "dp"))
    ep = ("x", "zb", "zi", "c")
    by_row = P(None, ("dp",) + ep, None)
    return jax.shard_map(
        on_device,
        mesh=fine,
        in_specs=(by_row, by_row, by_row, P(ep, None, None)),
        out_specs=by_row,
        check_vma=False,
    )
```

```python
import jax
import jax.numpy as jnp
from jax import lax
from jax.experimental import pallas as pl
from jax.experimental.pallas import tpu as pltpu
from jax.sharding import Mesh, PartitionSpec as P

FF = 1536
BF = jnp.bfloat16
F32 = jnp.float32
ROWS_OF = ("x", "zb")
HOME = ("x", "zb", "zi")
ANYWHERE = pl.BlockSpec(memory_space=pl.ANY)
NT = (((1,), (1,)), ((), ()))


def exchange(array, axis, step):
    size = lax.axis_size(axis)
    return lax.ppermute(array, axis, [(i, i ^ step) for i in range(size)])


def swap(array):
    return lax.ppermute(array, "c", [(0, 1), (1, 0)])


def named_in(ids, experts):
    rows = ids.shape[1]
    expert = lax.broadcasted_iota(jnp.int32, (experts, rows), 0)
    row = lax.broadcasted_iota(jnp.int32, (rows, rows), 0)
    earlier = (row < lax.broadcasted_iota(jnp.int32, (rows, rows), 1)).astype(F32)
    hits = [ids[k : k + 1] == expert for k in range(ids.shape[0])]
    named = jnp.zeros((experts, rows), jnp.bool_)
    for hit in hits:
        named = named | hit
    named = named.astype(F32)
    return hits, named, jnp.dot(named, earlier, preferred_element_type=F32)


def pack_kernel(ids_ref, tokens_ref, out_ref):
    batches, _, rows = ids_ref.shape
    experts, slots, width = out_ref.shape
    capacity = slots // batches
    count = experts * slots
    owner = lax.broadcasted_iota(jnp.int32, (count, experts), 0) // slots
    spread = (owner == lax.broadcasted_iota(jnp.int32, (count, experts), 1)).astype(F32)
    slot = lax.broadcasted_iota(jnp.int32, (count, rows), 0) % slots
    total = jnp.zeros((count, width), F32)
    for m in range(batches):
        _, named, before = named_in(ids_ref[m], experts)
        named = jnp.dot(spread, named, preferred_element_type=F32)
        before = jnp.dot(spread, before, preferred_element_type=F32)
        here = (slot // capacity == m) & (before == (slot % capacity).astype(F32))
        pick = ((named > 0.5) & here).astype(BF)
        total += jnp.dot(pick, tokens_ref[m], preferred_element_type=F32)
    out_ref[...] = total.astype(BF).reshape(out_ref.shape)


def whole(count):
    return [pl.BlockSpec(memory_space=pltpu.VMEM)] * count


def packed_of(expert_ids, tokens, experts, slots):
    return pl.pallas_call(
        pack_kernel,
        in_specs=whole(2),
        out_specs=whole(1)[0],
        out_shape=jax.ShapeDtypeStruct((experts, slots, tokens.shape[2]), BF),
        compiler_params=pltpu.CompilerParams(vmem_limit_bytes=16 << 20),
    )(expert_ids.transpose(0, 2, 1), tokens)


def repeat_kernel(_, *refs):
    arrays, out_ref, done = refs[:-2], refs[-2], refs[-1]
    copies = [
        pltpu.make_async_copy(ref, out_ref.at[copy, k], done.at[copy, k])
        for copy in range(out_ref.shape[0])
        for k, ref in enumerate(arrays)
    ]
    for copy in copies:
        copy.start()
    for copy in copies:
        copy.wait()


def repeat_after(earlier, arrays, times):
    return pl.pallas_call(
        repeat_kernel,
        in_specs=[ANYWHERE] + whole(len(arrays)),
        out_specs=pl.BlockSpec(memory_space=pltpu.HBM),
        out_shape=jax.ShapeDtypeStruct((times, len(arrays)) + arrays[0].shape, BF),
        scratch_shapes=[pltpu.SemaphoreType.DMA((times, len(arrays)))],
        compiler_params=pltpu.CompilerParams(vmem_limit_bytes=53 << 20),
    )(earlier, *arrays)


def copy_kernel(_, array_ref, out_ref):
    out_ref[...] = array_ref[...]


def copy_after(earlier, array):
    return pl.pallas_call(
        copy_kernel,
        in_specs=[ANYWHERE] + whole(1),
        out_specs=whole(1)[0],
        out_shape=jax.ShapeDtypeStruct(array.shape, array.dtype),
        compiler_params=pltpu.CompilerParams(vmem_limit_bytes=16 << 20),
    )(earlier, array)


def up_kernel(first_ref, second_ref, own_ref, other_ref, out_ref):
    units = own_ref.shape[0] // 3
    width = own_ref.shape[1]
    rows = [ref[...].reshape(-1, width) for ref in (first_ref, second_ref)]
    rows = jnp.concatenate(rows, axis=0)
    hidden = []
    for ref in (own_ref, other_ref):
        both = lax.dot_general(ref[: 2 * units], rows, NT, preferred_element_type=F32)
        gate = both[:units]
        hidden.append(gate / (1.0 + jnp.exp(-gate)) * both[units:])
    out_ref[...] = jnp.concatenate(hidden, axis=0).T.astype(BF)


def hidden_of(first, second, own, other):
    count = 2 * first.shape[0] * first.shape[1]
    both = own.shape[0] // 3 * 2
    return pl.pallas_call(
        up_kernel,
        grid=(1,),
        in_specs=whole(3) + [pl.BlockSpec((both, own.shape[1]), lambda i: (0, 0))],
        out_specs=whole(1)[0],
        out_shape=jax.ShapeDtypeStruct((count, both), BF),
        compiler_params=pltpu.CompilerParams(vmem_limit_bytes=24 << 20),
    )(first, second, own, other)


def down_kernel(place_ref, hidden_ref, shares_ref, ids_ref, gates_ref, out_ref, weights_ref):
    shares, cores, line = shares_ref.shape[:3]
    experts, _, slots, columns = out_ref.shape
    total = jnp.zeros((line * experts * slots, columns), F32)
    for at in range(line):
        k = place_ref[0] ^ at
        weights = [
            shares_ref[y, place_ref[1] ^ core, k] for core in range(cores) for y in range(shares)
        ]
        weights = jnp.concatenate(weights, axis=0)
        total += jnp.dot(hidden_ref[at], weights, preferred_element_type=F32)
    half = experts // 2
    total = total.astype(BF).reshape(2, line, half, slots, columns)
    for part in range(2):
        for p in range(line):
            out_ref[part * half : (part + 1) * half, p] = total[part, p]
    batches, capacity, _, rows = weights_ref.shape
    for m in range(batches):
        hits, _, before = named_in(ids_ref[m], experts)
        weight = jnp.zeros((experts, rows), F32)
        for k, hit in enumerate(hits):
            weight = jnp.where(hit, gates_ref[m, k : k + 1], weight)
        for s in range(capacity):
            weights_ref[m, s] = jnp.where(before == s, weight, 0.0)


def outputs_of(place, hidden, shares, expert_ids, gate_scores, experts, slots):
    batches, rows, _ = expert_ids.shape
    return pl.pallas_call(
        down_kernel,
        in_specs=[pl.BlockSpec(memory_space=pltpu.SMEM)] + whole(4),
        out_specs=whole(2),
        out_shape=[
            jax.ShapeDtypeStruct((experts, hidden.shape[0], slots, shares.shape[-1]), BF),
            jax.ShapeDtypeStruct((batches, slots // batches, experts, rows), F32),
        ],
        compiler_params=pltpu.CompilerParams(vmem_limit_bytes=16 << 20),
    )(place, hidden, shares, expert_ids.transpose(0, 2, 1), gate_scores.transpose(0, 2, 1))


def on_device(tokens, expert_ids, gate_scores, expert_weights):
    batches, row_count, width = tokens.shape
    experts = lax.axis_size("x") * lax.axis_size("zb")
    line = lax.axis_size("zi")
    capacity = 2
    slots = batches * capacity
    columns = width // line
    turned = expert_weights[0].T
    units = turned.shape[0] // 3
    place = lax.axis_index("zi")
    share = units // lax.axis_size("dp")
    down = lax.dynamic_slice_in_dim(turned, 2 * units + share * lax.axis_index("dp"), share, 0)
    down = down.reshape(share, line, columns)

    def for_place(at):
        return lax.dynamic_index_in_dim(down, at, 1, keepdims=False)

    pieces = [for_place(place)] + [exchange(for_place(place ^ k), "zi", k) for k in range(1, line)]
    packed = packed_of(expert_ids, tokens, experts, slots)
    mark = packed[0, 0, 0]
    up = jnp.where(mark == mark, turned[: 2 * units], jnp.zeros((), BF))
    other = swap(up)
    arrived = lax.all_to_all(packed, ROWS_OF, split_axis=0, concat_axis=0, tiled=True)
    replicas, cores = lax.axis_size("dp"), lax.axis_size("c")
    shares = repeat_after(arrived, pieces, replicas * cores)
    shares = lax.all_to_all(shares, ("dp", "c"), split_axis=0, concat_axis=0, tiled=True)
    shares = shares.reshape((replicas, cores) + shares.shape[1:])
    half = experts // 2
    first = lax.all_gather(arrived[:half], "zi", axis=0, tiled=True)
    later = copy_after(first, arrived[half:])
    second = lax.all_gather(later, "zi", axis=0, tiled=True)
    hidden = hidden_of(first, second, turned, other)
    gathered = lax.all_gather(hidden, "zi", axis=0)
    position = jnp.stack([place, lax.axis_index("c")]).astype(jnp.int32)
    done, weighting = outputs_of(
        position, gathered, shares, expert_ids, gate_scores, experts, slots
    )
    done = done.reshape(experts * line, slots, columns)
    returned = lax.all_to_all(done, HOME, split_axis=0, concat_axis=0, tiled=True)
    returned = returned.reshape(experts, line, batches, capacity, columns).astype(F32)
    mixed = jnp.einsum("mser,ezmsd->mrzd", weighting, returned, precision=lax.Precision.HIGHEST)
    return mixed.astype(BF).reshape(batches, row_count, width)


def solution(mesh):
    fine = Mesh(mesh.devices.reshape(4, 4, 4, 2, 4), ("x", "zb", "zi", "c", "dp"))
    ep = ("x", "zb", "zi", "c")
    by_row = P(None, ("dp",) + ep, None)
    return jax.shard_map(
        on_device,
        mesh=fine,
        in_specs=(by_row, by_row, by_row, P(ep, None, None)),
        out_specs=by_row,
        check_vma=False,
    )
```

```python
import jax
import jax.numpy as jnp
from jax import lax
from jax.experimental import pallas as pl
from jax.experimental.pallas import tpu as pltpu
from jax.sharding import Mesh, PartitionSpec as P

FF = 1536
BF = jnp.bfloat16
F32 = jnp.float32
ROWS_OF = ("x", "zb")
HOME = ("x", "zb", "zi")
ANYWHERE = pl.BlockSpec(memory_space=pl.ANY)
NT = (((1,), (1,)), ((), ()))


def exchange(array, axis, step):
    size = lax.axis_size(axis)
    return lax.ppermute(array, axis, [(i, i ^ step) for i in range(size)])


def swap(array):
    return lax.ppermute(array, "c", [(0, 1), (1, 0)])


def named_in(ids, experts):
    rows = ids.shape[1]
    expert = lax.broadcasted_iota(jnp.int32, (experts, rows), 0)
    row = lax.broadcasted_iota(jnp.int32, (rows, rows), 0)
    earlier = (row < lax.broadcasted_iota(jnp.int32, (rows, rows), 1)).astype(F32)
    hits = [ids[k : k + 1] == expert for k in range(ids.shape[0])]
    named = jnp.zeros((experts, rows), jnp.bool_)
    for hit in hits:
        named = named | hit
    named = named.astype(F32)
    return hits, named, jnp.dot(named, earlier, preferred_element_type=F32)


def pack_kernel(ids_ref, tokens_ref, out_ref):
    batches, _, rows = ids_ref.shape
    experts, slots, width = out_ref.shape
    capacity = slots // batches
    count = experts * slots
    owner = lax.broadcasted_iota(jnp.int32, (count, experts), 0) // slots
    spread = (owner == lax.broadcasted_iota(jnp.int32, (count, experts), 1)).astype(F32)
    slot = lax.broadcasted_iota(jnp.int32, (count, rows), 0) % slots
    total = jnp.zeros((count, width), F32)
    for m in range(batches):
        _, named, before = named_in(ids_ref[m], experts)
        named = jnp.dot(spread, named, preferred_element_type=F32)
        before = jnp.dot(spread, before, preferred_element_type=F32)
        here = (slot // capacity == m) & (before == (slot % capacity).astype(F32))
        pick = ((named > 0.5) & here).astype(BF)
        total += jnp.dot(pick, tokens_ref[m], preferred_element_type=F32)
    out_ref[...] = total.astype(BF).reshape(out_ref.shape)


def whole(count):
    return [pl.BlockSpec(memory_space=pltpu.VMEM)] * count


def packed_of(expert_ids, tokens, experts, slots):
    return pl.pallas_call(
        pack_kernel,
        in_specs=whole(2),
        out_specs=whole(1)[0],
        out_shape=jax.ShapeDtypeStruct((experts, slots, tokens.shape[2]), BF),
        compiler_params=pltpu.CompilerParams(vmem_limit_bytes=16 << 20),
    )(expert_ids.transpose(0, 2, 1), tokens)


def repeat_kernel(_, *refs):
    arrays, out_ref, done = refs[:-2], refs[-2], refs[-1]
    copies = [
        pltpu.make_async_copy(ref, out_ref.at[copy, k], done.at[copy, k])
        for copy in range(out_ref.shape[0])
        for k, ref in enumerate(arrays)
    ]
    for copy in copies:
        copy.start()
    for copy in copies:
        copy.wait()


def repeat_after(earlier, arrays, times):
    return pl.pallas_call(
        repeat_kernel,
        in_specs=[ANYWHERE] + whole(len(arrays)),
        out_specs=pl.BlockSpec(memory_space=pltpu.HBM),
        out_shape=jax.ShapeDtypeStruct((times, len(arrays)) + arrays[0].shape, BF),
        scratch_shapes=[pltpu.SemaphoreType.DMA((times, len(arrays)))],
        compiler_params=pltpu.CompilerParams(vmem_limit_bytes=53 << 20),
    )(earlier, *arrays)


def copy_kernel(_, array_ref, out_ref):
    out_ref[...] = array_ref[...]


def copy_after(earlier, array):
    return pl.pallas_call(
        copy_kernel,
        in_specs=[ANYWHERE] + whole(1),
        out_specs=whole(1)[0],
        out_shape=jax.ShapeDtypeStruct(array.shape, array.dtype),
        compiler_params=pltpu.CompilerParams(vmem_limit_bytes=16 << 20),
    )(earlier, array)


def up_kernel(first_ref, second_ref, own_ref, other_ref, out_ref):
    units = own_ref.shape[0] // 3
    width = own_ref.shape[1]
    rows = [ref[...].reshape(-1, width) for ref in (first_ref, second_ref)]
    rows = jnp.concatenate(rows, axis=0)
    hidden = []
    for ref in (own_ref, other_ref):
        both = lax.dot_general(ref[: 2 * units], rows, NT, preferred_element_type=F32)
        gate = both[:units]
        hidden.append(gate / (1.0 + jnp.exp(-gate)) * both[units:])
    out_ref[...] = jnp.concatenate(hidden, axis=0).T.astype(BF)


def hidden_of(first, second, own, other):
    count = 2 * first.shape[0] * first.shape[1]
    both = own.shape[0] // 3 * 2
    return pl.pallas_call(
        up_kernel,
        grid=(1,),
        in_specs=whole(3) + [pl.BlockSpec((both, own.shape[1]), lambda i: (0, 0))],
        out_specs=whole(1)[0],
        out_shape=jax.ShapeDtypeStruct((count, both), BF),
        compiler_params=pltpu.CompilerParams(vmem_limit_bytes=24 << 20),
    )(first, second, own, other)


def down_kernel(place_ref, hidden_ref, shares_ref, ids_ref, gates_ref, out_ref, weights_ref):
    shares, cores, line = shares_ref.shape[:3]
    experts, _, slots, columns = out_ref.shape
    total = jnp.zeros((line * experts * slots, columns), F32)
    for at in range(line):
        k = place_ref[0] ^ at
        weights = [
            shares_ref[y, place_ref[1] ^ core, k] for core in range(cores) for y in range(shares)
        ]
        weights = jnp.concatenate(weights, axis=0)
        total += jnp.dot(hidden_ref[at], weights, preferred_element_type=F32)
    half = experts // 2
    total = total.astype(BF).reshape(2, line, half, slots, columns)
    for part in range(2):
        for p in range(line):
            out_ref[part * half : (part + 1) * half, p] = total[part, p]
    batches, capacity, _, rows = weights_ref.shape
    for m in range(batches):
        hits, _, before = named_in(ids_ref[m], experts)
        weight = jnp.zeros((experts, rows), F32)
        for k, hit in enumerate(hits):
            weight = jnp.where(hit, gates_ref[m, k : k + 1], weight)
        for s in range(capacity):
            weights_ref[m, s] = jnp.where(before == s, weight, 0.0)


def outputs_of(place, hidden, shares, expert_ids, gate_scores, experts, slots):
    batches, rows, _ = expert_ids.shape
    return pl.pallas_call(
        down_kernel,
        in_specs=[pl.BlockSpec(memory_space=pltpu.SMEM)] + whole(4),
        out_specs=whole(2),
        out_shape=[
            jax.ShapeDtypeStruct((experts, hidden.shape[0], slots, shares.shape[-1]), BF),
            jax.ShapeDtypeStruct((batches, slots // batches, experts, rows), F32),
        ],
        compiler_params=pltpu.CompilerParams(vmem_limit_bytes=16 << 20),
    )(place, hidden, shares, expert_ids.transpose(0, 2, 1), gate_scores.transpose(0, 2, 1))


def on_device(tokens, expert_ids, gate_scores, expert_weights):
    batches, row_count, width = tokens.shape
    experts = lax.axis_size("x") * lax.axis_size("zb")
    line = lax.axis_size("zi")
    capacity = 2
    slots = batches * capacity
    columns = width // line
    turned = expert_weights[0].T
    units = turned.shape[0] // 3
    place = lax.axis_index("zi")
    share = units // lax.axis_size("dp")
    down = lax.dynamic_slice_in_dim(turned, 2 * units + share * lax.axis_index("dp"), share, 0)
    down = down.reshape(share, line, columns)

    def for_place(at):
        return lax.dynamic_index_in_dim(down, at, 1, keepdims=False)

    pieces = [for_place(place)] + [exchange(for_place(place ^ k), "zi", k) for k in range(1, line)]
    packed = packed_of(expert_ids, tokens, experts, slots)
    other = swap(turned)
    arrived = lax.all_to_all(packed, ROWS_OF, split_axis=0, concat_axis=0, tiled=True)
    replicas, cores = lax.axis_size("dp"), lax.axis_size("c")
    shares = repeat_after(arrived, pieces, replicas * cores)
    shares = lax.all_to_all(shares, ("dp", "c"), split_axis=0, concat_axis=0, tiled=True)
    shares = shares.reshape((replicas, cores) + shares.shape[1:])
    half = experts // 2
    first = lax.all_gather(arrived[:half], "zi", axis=0, tiled=True)
    later = copy_after(first, arrived[half:])
    second = lax.all_gather(later, "zi", axis=0, tiled=True)
    hidden = hidden_of(first, second, turned, other)
    gathered = lax.all_gather(hidden, "zi", axis=0)
    position = jnp.stack([place, lax.axis_index("c")]).astype(jnp.int32)
    done, weighting = outputs_of(
        position, gathered, shares, expert_ids, gate_scores, experts, slots
    )
    done = done.reshape(experts * line, slots, columns)
    returned = lax.all_to_all(done, HOME, split_axis=0, concat_axis=0, tiled=True)
    returned = returned.reshape(experts, line, batches, capacity, columns).astype(F32)
    mixed = jnp.einsum("mser,ezmsd->mrzd", weighting, returned, precision=lax.Precision.HIGHEST)
    return mixed.astype(BF).reshape(batches, row_count, width)


def solution(mesh):
    fine = Mesh(mesh.devices.reshape(4, 4, 4, 2, 4), ("x", "zb", "zi", "c", "dp"))
    ep = ("x", "zb", "zi", "c")
    by_row = P(None, ("dp",) + ep, None)
    return jax.shard_map(
        on_device,
        mesh=fine,
        in_specs=(by_row, by_row, by_row, P(ep, None, None)),
        out_specs=by_row,
        check_vma=False,
    )
```
